32 devices in a mesh: groups: 2 (over y), seq: 8 (over z, x), chan: 2 (over core).
Axes of the slice: x: 2, y: 2, z: 4, core: 2. Of those that a mesh axis runs over, the one named last changes fastest.
Arguments:
- inputs: bfloat16 [4096, 8192], P(('groups', 'seq'), 'chan'), parts along dimension 0, may hold values from -6 to 6
- bounds: int32 [16], P(('groups', 'seq')), parts along dimension 0, may hold values from 0 to 256, as said below
- feat_first: float32 [3, 3, 8192], P(None, None, 'chan'), may hold values from -4 to 4
- li_decay: float32 [16, 16], P('chan'), may hold values from 0 to 1
- li_residue: float32 [16, 16], P('chan'), may hold values from -4 to 4
- feat_second: float32 [3, 3, 8192], P(None, None, 'chan'), may hold values from -4 to 4
- mr_filter: bfloat16 [16, 128], P('chan'), may hold values from -0.5 to 0.5
Outputs:
- mixed: bfloat16 [4096, 8192], P(('groups', 'seq'), 'chan'), parts along dimension 0
The draws below stay inside these ranges and needn't reach their ends.
There are 2 independent parts, one for each index of `groups`. The reference program is written for one: setup_inputs(seed, part) draws one part's arguments, and reference() takes and returns one part's arrays. A program takes and returns all parts, laid end to end along the dimension named above; an argument that names none is the same for every part. Nothing has to cross between parts.
Inputs may be any that keep to these rules, and one draw needn't show every extreme that they name: bounds[s] is the position within block s where a document begins; 256 means no document begins in that block.
All inputs are finite; a program needn't handle non-finite values.
Results may differ from the reference program's by a relative error of at most 0.0081.
Values may be sent and summed in bfloat16 or wider, within the bound.
No kernel may reach another device: no remote copies, remote signals or barrier semaphores. Data moves between devices by JAX's collectives and lax.ppermute only.
A program may use at most 192 MiB of HBM per device.

```python
import math
import jax
import jax.numpy as jnp
from jax import lax

D = 8192
GROUP = 512
MODES = 16
MR_LEN = 128
TOK_DEV = 256
FG = 16
SHARDS = 8
LENGTH = 2048


def draw_bounds(key, part):
    key = jax.random.fold_in(key, 3)
    key = jax.random.fold_in(key, part)
    first_key, second_key, third_key = jax.random.split(key, 3)
    position = jax.random.randint(first_key, (SHARDS,), 0, TOK_DEV)
    chosen = jax.random.randint(second_key, (SHARDS,), 0, 16) == 0
    result = jnp.where(chosen, position, TOK_DEV)
    picked = jax.random.randint(third_key, (), 0, SHARDS)
    result = result.at[picked].set(0)
    result = result.at[(picked + 1) % SHARDS].set(TOK_DEV)
    return result.astype(jnp.int32)


def draw_li_decay(key, part):
    key = jax.random.fold_in(key, 7)
    first_key, second_key, third_key = jax.random.split(key, 3)
    slow_top = math.log(10.0) / LENGTH
    slow_rate = slow_top * jnp.exp(jax.random.uniform(first_key, (FG, MODES), jnp.float32, math.log(0.05), 0.0))
    fast_rate = jnp.exp(jax.random.uniform(second_key, (FG, MODES), jnp.float32, math.log(1.0 / 50.0), math.log(1.0 / 20.0)))
    share = 0.5
    picked = jax.random.uniform(third_key, (FG, MODES), jnp.float32) < share
    return jnp.where(picked, fast_rate, slow_rate).astype(jnp.float32)


def level_of(rng, shape, cuts, low, high):
    def one(dim, blocks):
        steps = jax.random.uniform(jax.random.fold_in(jax.random.fold_in(rng, 6), dim), (blocks,), jnp.float32, low / len(cuts), high / len(cuts))
        return jnp.repeat(jnp.exp(steps), shape[dim] // blocks).reshape((-1,) + (1,) * (len(shape) - dim - 1))

    level = one(*cuts[0])
    for cut in cuts[1:]:
        level = level * one(*cut)
    return level


def gaussian(rng, dims, deviation, reach, pieces=(), kind=jnp.bfloat16):
    array = jax.random.normal(rng, dims, jnp.float32) * deviation
    if len(pieces) > 0:
        array = level_of(rng, dims, pieces, -0.22, 0.18) * array
    return jnp.clip(array, min=-reach, max=reach).astype(kind)


def setup_inputs(seed: int = 0, part: int = 0) -> dict:
    arg_keys = jax.random.split(jax.random.key(seed), 8)
    own_keys = jax.random.split(jax.random.fold_in(arg_keys[7], part), 8)
    inputs = gaussian(own_keys[0], (LENGTH, D), 1.0, 6.0, ((0, 8), (1, 2)))
    bounds = draw_bounds(jax.random.fold_in(jax.random.fold_in(arg_keys[7], part), 71), part)
    feat_first = gaussian(arg_keys[2], (3, 3, D), 0.6, 4.0, ((2, 2),), jnp.float32)
    li_decay = draw_li_decay(jax.random.fold_in(arg_keys[7], 71), part)
    li_residue = gaussian(arg_keys[4], (FG, MODES), 1.0, 4.0, ((0, 2),), jnp.float32)
    feat_second = gaussian(arg_keys[5], (3, 3, D), 0.6, 4.0, ((2, 2),), jnp.float32)
    mr_filter = gaussian(arg_keys[6], (FG, MR_LEN), MR_LEN ** -0.5, 0.5, ((0, 2),))
    return dict(inputs=inputs, bounds=bounds, feat_first=feat_first, li_decay=li_decay, li_residue=li_residue, feat_second=feat_second, mr_filter=mr_filter)


PRECISE = lax.Precision.HIGHEST

def features(extended, ext_counts, weights, rows_out):
    target = ext_counts[2:2 + rows_out]
    outputs = []
    for branch in range(3):
        summed = jnp.zeros((rows_out, extended.shape[1]), jnp.float32)
        for offset in range(3):
            shifted = extended[2 - offset:2 - offset + rows_out].astype(jnp.float32)
            agrees = (ext_counts[2 - offset:2 - offset + rows_out] == target).astype(jnp.float32)
            summed = summed + weights[branch, offset] * shifted * agrees[:, None]
        outputs.append(summed)
    return (outputs[0], outputs[1], outputs[2])

def reference(inputs, bounds, feat_first, li_decay, li_residue, feat_second, mr_filter):
    where_at = jnp.arange(SHARDS, dtype=jnp.int32) * TOK_DEV + jnp.minimum(bounds, TOK_DEV - 1).astype(jnp.int32)
    starts = jnp.zeros((LENGTH,), jnp.int32).at[where_at].add((bounds < TOK_DEV).astype(jnp.int32))
    running = jnp.cumsum(starts).astype(jnp.int32)
    blocks = inputs.reshape(SHARDS, TOK_DEV, D)
    block_counts = running.reshape(SHARDS, TOK_DEV)
    decays = li_decay
    mode_weight = li_residue * jnp.sqrt(-jnp.expm1(-2.0 * decays)) / math.sqrt(MODES)
    lag_pos = jnp.arange(TOK_DEV).astype(jnp.float32)
    kernel = lax.optimization_barrier(jnp.sum(mode_weight[:, :, None] * jnp.exp(-decays[:, :, None] * lag_pos), axis=1))
    differ = jnp.arange(TOK_DEV, dtype=jnp.int32)[:, None] - jnp.arange(TOK_DEV, dtype=jnp.int32)[None, :]
    toeplitz = jnp.where(differ >= 0, kernel[:, jnp.clip(differ, 0, TOK_DEV - 1)], 0.0)
    rise_weight = jnp.exp(-decays[:, :, None] * (lag_pos + 1.0)) * mode_weight[:, :, None]
    end_decay = jnp.exp(-decays[:, :, None] * (TOK_DEV - 1.0 - lag_pos))
    through = jnp.exp(-decays * TOK_DEV)[:, :, None]

    def first_layer(carried_in, inputs_here):
        edge_rows, edge_counts, modal_state = carried_in
        rows_here, counts_here = inputs_here
        extended = jnp.concatenate([edge_rows, rows_here], 0)
        ext_counts = jnp.concatenate([edge_counts, counts_here])
        query_gate, key_part, value_part = features(extended, ext_counts, feat_first, TOK_DEV)
        mixed_in = (key_part * value_part).astype(jnp.bfloat16)
        mixed_wide = lax.optimization_barrier(mixed_in).astype(jnp.float32).reshape(TOK_DEV, FG, GROUP)
        agrees = (counts_here[:, None] == counts_here[None, :]).astype(jnp.float32)
        near_part = jnp.einsum('gtp,pgc->tgc', toeplitz * agrees, mixed_wide, precision=PRECISE)
        before = (counts_here == edge_counts[-1]).astype(jnp.float32)
        far_part = jnp.einsum('gmt,gmc->tgc', rise_weight * before, modal_state, precision=PRECISE)
        output = (query_gate * (near_part + far_part).reshape(TOK_DEV, D)).astype(jnp.bfloat16)
        reaches_end = (counts_here == counts_here[-1]).astype(jnp.float32)
        no_start = (counts_here[-1] == edge_counts[-1]).astype(jnp.float32)
        modal_state = no_start * through * modal_state + jnp.einsum('gmp,pgc->gmc', end_decay * reaches_end, mixed_wide, precision=PRECISE)
        return ((rows_here[-2:], counts_here[-2:], modal_state), output)
    start_carry = (jnp.zeros((2, D), inputs.dtype), jnp.zeros((2,), jnp.int32), jnp.zeros((FG, MODES, GROUP), jnp.float32))
    final_carry, first_out = lax.scan(first_layer, start_carry, (blocks, block_counts))
    span_all = TOK_DEV + MR_LEN - 1
    lag_taps = jnp.arange(TOK_DEV, dtype=jnp.int32)[:, None] + (MR_LEN - 1) - jnp.arange(span_all, dtype=jnp.int32)[None, :]
    inside = (lag_taps >= 0) & (lag_taps < MR_LEN)
    band_taps = jnp.where(inside, mr_filter.astype(jnp.float32)[:, jnp.clip(lag_taps, 0, MR_LEN - 1)], 0.0)

    def second_layer(carried_in, inputs_here):
        prior_rows, prior_counts = carried_in
        rows_here, counts_here = inputs_here
        extended = jnp.concatenate([prior_rows, rows_here], 0)
        ext_counts = jnp.concatenate([prior_counts, counts_here])
        query_two, key_two, value_two = features(extended, ext_counts, feat_second, span_all)
        product = (key_two * value_two).astype(jnp.bfloat16)
        product_wide = lax.optimization_barrier(product).astype(jnp.float32).reshape(span_all, FG, GROUP)
        agrees = (counts_here[:, None] == ext_counts[2:][None, :]).astype(jnp.float32)
        conv_out = jnp.einsum('gtp,pgc->tgc', band_taps * agrees, product_wide, precision=PRECISE)
        output = (query_two[MR_LEN - 1:] * conv_out.reshape(TOK_DEV, D)).astype(jnp.bfloat16)
        return ((extended[-(MR_LEN + 1):], ext_counts[-(MR_LEN + 1):]), output)
    second_start = (jnp.zeros((MR_LEN + 1, D), jnp.bfloat16), jnp.zeros((MR_LEN + 1,), jnp.int32))
    final_two, second_out = lax.scan(second_layer, second_start, (first_out, block_counts))
    return second_out.reshape(LENGTH, D)
```

```python
import functools
import math

import jax
import jax.numpy as jnp
from jax import lax
from jax.experimental import pallas as pl
from jax.experimental.pallas import tpu as pltpu
from jax.sharding import PartitionSpec as P

F32 = jnp.float32
BF = jnp.bfloat16
WIN = 144
LANE = 128
SMEM = pltpu.SMEM


def dot(a, b):
    return lax.dot_general(a, b, (((1,), (0,)), ((), ())), preferred_element_type=F32)


def iota(shape, dim):
    return lax.broadcasted_iota(jnp.int32, shape, dim)


def column(row):
    n = row.shape[1]
    return jnp.sum(
        jnp.where(iota((n, n), 0) == iota((n, n), 1), row, 0.0), axis=1, keepdims=True
    )


def one(cond):
    return jnp.where(cond, 1.0, 0.0).astype(BF)


def shift_matrix(rows, by, start):
    t, p = iota((rows, rows), 0), iota((rows, rows), 1)
    return one((p == t - by) & ((p >= start) == (t >= start)))


def combine(w, branch, taps):
    total = w[branch, 0:1, :] * taps[0]
    for o in (1, 2):
        total = total + w[branch, o : o + 1, :] * taps[o]
    return total


def first_taps(x, edge, s1, s2, own, prior, length):
    lanes = x.shape[1]
    x1, x2 = dot(s1, x), dot(s2, x)
    row = iota((16, lanes), 0)
    e0, e1 = edge[0:1].astype(F32), edge[1:2].astype(F32)
    m10 = jnp.where(own == 0, 0.0, 1.0)
    m20 = jnp.where((own == 0) | (prior == length - 1), 0.0, 1.0)
    m21 = jnp.where((own == 0) | (own == 1), 0.0, 1.0)
    add1 = jnp.where(row == 0, e1 * m10, 0.0)
    add2 = jnp.where(row == 0, e0 * m20, 0.0) + jnp.where(row == 1, e1 * m21, 0.0)
    x1 = jnp.concatenate([x1[:16] + add1, x1[16:]], 0)
    x2 = jnp.concatenate([x2[:16] + add2, x2[16:]], 0)
    return x.astype(F32), x1, x2


def split(v):
    hi = v.astype(BF)
    return hi, (v - hi.astype(F32)).astype(BF)


def states_kernel(cut, modes, scal, x_ref, edge_ref, w_ref, dec_ref, out_ref, sh_ref):
    g = pl.program_id(0)
    length, lanes = x_ref.shape
    own, prior = scal[0], scal[1]

    @pl.when(g == 0)
    def _():
        sh_ref[0] = shift_matrix(length, 1, own)
        sh_ref[1] = shift_matrix(length, 2, own)
        flag = jnp.full((2 * modes, LANE), own, jnp.int32).astype(F32)
        out_ref[:, pl.ds(out_ref.shape[1] - LANE, LANE)] = flag.astype(BF)

    taps = first_taps(x_ref[...], edge_ref[...], sh_ref[0], sh_ref[1], own, prior, length)
    u = (combine(w_ref, 1, taps) * combine(w_ref, 2, taps)).astype(BF)
    dec = column(dec_ref[pl.ds(g, 1), :])
    p = iota((modes, length), 1)
    lag = (length - 1 - p).astype(F32)
    full = jnp.where((p >= own) | (own >= length), jnp.exp(-dec * lag), 0.0)
    lag = jnp.maximum(cut - 1 - p, 0).astype(F32)
    part = jnp.where(
        (p < cut) & ((p >= own) | (own >= cut)), jnp.exp(-dec * lag), 0.0
    )
    hi, lo = split(jnp.concatenate([full, part], 0))
    both = dot(jnp.concatenate([hi, lo], 0), u)
    state = both[: 2 * modes] + both[2 * modes :]
    out_ref[:, pl.ds(pl.multiple_of(g * lanes, lanes), lanes)] = state.astype(BF)


def pair_kernel(cut, modes, length, scal, mine_ref, other_ref, dec_ref, out_ref):
    groups = dec_ref.shape[0]
    width = mine_ref.shape[1] - LANE
    lanes = width // groups
    even = scal[2] == 0
    end = slice(width, width + LANE)

    def pick(rows, cols):
        a = mine_ref[rows, cols].astype(F32)
        b = other_ref[rows, cols].astype(F32)
        return jnp.where(even, a, b), jnp.where(even, b, a)

    top, low = slice(0, modes), slice(modes, 2 * modes)
    f_bound, s_bound = pick(top, end)
    free_f = jnp.where(f_bound >= length, 1.0, 0.0)
    free_s = jnp.where(s_bound >= length, 1.0, 0.0)
    free_c = jnp.where(s_bound >= cut, 1.0, 0.0)
    out_ref[top, end] = (free_f * free_s).astype(BF)
    out_ref[low, end] = (free_f * free_c).astype(BF)
    for g in range(groups):
        cols = slice(g * lanes, (g + 1) * lanes)
        dec = column(dec_ref[g : g + 1, :])
        f_full, s_full = pick(top, cols)
        _, s_part = pick(low, cols)
        out_ref[top, cols] = (
            s_full + jnp.exp(-dec * length) * free_s[:, :1] * f_full
        ).astype(BF)
        out_ref[low, cols] = (
            s_part + jnp.exp(-dec * cut) * free_c[:, :1] * f_full
        ).astype(BF)


def carry_kernel(cut, modes, length, scal, other_ref, near_ref, dec_ref, *refs):
    far, (own_ref, win_ref) = refs[:-2], refs[-2:]
    groups = dec_ref.shape[0]
    width = other_ref.shape[1] - LANE
    lanes = width // groups
    even = scal[2] == 0
    prior = scal[1]
    end = slice(width, width + 1)
    top, low = slice(0, modes), slice(modes, 2 * modes)
    near_free = near_ref[top, width : width + LANE].astype(F32)[:, :1]
    near_part = near_ref[low, width : width + LANE].astype(F32)[:, :1]
    far_free = [f[:, width : width + LANE].astype(F32)[:, :1] for f in far]
    pass_own = jnp.where(prior >= length, 1.0, 0.0)
    pass_cut = jnp.where(prior >= cut, 1.0, 0.0)
    for g in range(groups):
        cols = slice(g * lanes, (g + 1) * lanes)
        dec = column(dec_ref[g : g + 1, :])
        pair = jnp.exp(-dec * (2 * length))
        behind = jnp.zeros((modes, lanes), F32)
        for f, free in zip(far[::-1], far_free[::-1]):
            behind = f[:, cols].astype(F32) + pair * free * behind
        whole = near_ref[top, cols].astype(F32) + pair * near_free * behind
        odd_own = other_ref[top, cols].astype(F32) + jnp.exp(-dec * length) * pass_own * whole
        odd_win = other_ref[low, cols].astype(F32) + jnp.exp(-dec * cut) * pass_cut * whole
        even_win = near_ref[low, cols].astype(F32) + (
            jnp.exp(-dec * (cut + length)) * near_part * behind
        )
        own = jnp.where(even, whole, odd_own)
        win = jnp.where(even, even_win, odd_win)
        for ref, v in ((own_ref, own), (win_ref, win)):
            hi, lo = split(v)
            ref[:, cols] = jnp.concatenate([hi, lo, hi], 0)


def tables_kernel(cut, modes, length, scal, dec_ref, res_ref, mr_ref, *outs):
    t_own, t_win, r_own, r_win, b_own, b_win, b_head = outs
    g = pl.program_id(0)
    own, prior = scal[0], scal[1]
    wide = 2 * length
    base = length - WIN
    dec_row = dec_ref[pl.ds(g, 1), :]
    weight_row = res_ref[pl.ds(g, 1), :] * jnp.sqrt(
        jnp.maximum(1.0 - jnp.exp(-2.0 * dec_row), 0.0)
    ) / math.sqrt(modes)
    small = 2.0 * dec_row
    series = small * (1.0 - small * (0.5 - small * (1.0 / 6 - small * (1.0 / 24))))
    weight_row = jnp.where(
        small < 0.05,
        res_ref[pl.ds(g, 1), :] * jnp.sqrt(series) / math.sqrt(modes),
        weight_row,
    )
    dec, weight = column(dec_row), column(weight_row)
    back = iota((modes, wide), 1)
    back = jnp.where(back == 0, 0, wide - back).astype(F32)
    taps = jnp.sum(weight * jnp.exp(-dec * back), axis=0, keepdims=True)
    full = pltpu.roll(jnp.broadcast_to(taps, (length, wide)), 0, 1, stride=1, stride_axis=0)
    t, p = iota((length, length), 0), iota((length, length), 1)
    seen = (p <= t) & ((p >= own) == (t >= own))
    t_own[...] = jnp.where(seen, full[:, :length], 0.0).astype(BF)
    tw, pw = iota((WIN, WIN), 0) + base, iota((WIN, WIN), 1) + base
    seen = (pw <= tw) & (pw >= cut) & ((pw >= prior) == (tw >= prior))
    t_win[...] = jnp.where(seen, full[:WIN, :WIN], 0.0).astype(BF)

    tl = iota((modes, length), 1)
    rise = jnp.where(tl < own, weight * jnp.exp(-dec * (tl + 1).astype(F32)), 0.0)
    wl = tl + base
    lag = jnp.maximum(wl - cut + 1, 0)
    fits = (wl >= cut) & ((prior < cut) | (prior > wl))
    rise_w = jnp.where(fits, weight * jnp.exp(-dec * lag.astype(F32)), 0.0)
    for ref, v, rows in ((r_own, rise, length), (r_win, rise_w, WIN)):
        hi = v.astype(BF).astype(F32)
        stack = jnp.concatenate([hi, hi, v - hi, jnp.zeros((LANE - 3 * modes, length), F32)], 0)
        ref[...] = jnp.transpose(stack)[:rows, : 3 * modes].astype(BF)

    count = mr_ref.shape[1]
    o, n = iota((count, wide), 0), iota((count, wide), 1)
    back = dot(mr_ref[...], one(((n == 0) & (o == 0)) | ((n > 0) & (wide - n == o))))
    band = pltpu.roll(
        jnp.broadcast_to(back, (2 * WIN, wide)), 0, 1, stride=1, stride_axis=0
    )
    seen = (p <= t) & ((p >= own) == (t >= own))
    here = jnp.where(seen, band[:length, :length], 0.0)
    b_own[...] = jnp.where(p >= 2, here, 0.0).astype(BF)
    b_head[...] = jnp.where(p >= 2, 0.0, here)[:WIN, :16].astype(BF)
    tb, pb = iota((WIN, WIN), 0), iota((WIN, WIN), 1) + base
    seen = (tb < own) & ((prior >= length) | (pb >= prior))
    b_win[...] = jnp.where(seen, band[WIN : 2 * WIN, :WIN], 0.0).astype(BF)


def own_kernel(
    scal, x_ref, edge_ref, w1_ref, w2_ref, t_ref, r_ref, b_ref, st_ref,
    out_ref, z_ref, q_ref, y_ref, sh_ref,
):
    g = pl.program_id(0)
    length, lanes = x_ref.shape
    own, prior = scal[0], scal[1]

    @pl.when(g == 0)
    def _():
        sh_ref[0] = shift_matrix(length, 1, own)
        sh_ref[1] = shift_matrix(length, 2, own)

    taps = first_taps(x_ref[...], edge_ref[...], sh_ref[0], sh_ref[1], own, prior, length)
    u = (combine(w1_ref, 1, taps) * combine(w1_ref, 2, taps)).astype(BF)
    z = dot(t_ref[...], u) + dot(r_ref[...], st_ref[...])
    y = (combine(w1_ref, 0, taps) * z).astype(BF)
    y_ref[...] = y[:16]
    taps = (y.astype(F32), dot(sh_ref[0], y), dot(sh_ref[1], y))
    w = (combine(w2_ref, 1, taps) * combine(w2_ref, 2, taps)).astype(BF)
    z = dot(b_ref[...], w)
    q = combine(w2_ref, 0, taps)
    z_ref[...] = z[:WIN]
    q_ref[...] = q[:WIN]
    out_ref[...] = (q * z).astype(BF)


def head_kernel(
    scal, tail_ref, w1_ref, w2_ref, t_ref, r_ref, b_ref, bh_ref, st_ref, z_ref, q_ref, y_ref,
    old_ref, out_ref, length,
):
    del old_ref
    rows, lanes = tail_ref.shape
    own, prior = scal[0], scal[1]
    base = length - WIN
    i, k = iota((WIN, rows), 0), iota((WIN, rows), 1)
    tb, pb = i + base, k + (length - rows)
    taps = []
    for o in range(3):
        m = one((pb == tb - o) & ((pb >= prior) == (tb >= prior)))
        taps.append(dot(m, tail_ref[...]))
    u = (combine(w1_ref, 1, taps) * combine(w1_ref, 2, taps)).astype(BF)
    z = dot(t_ref[...], u) + dot(r_ref[...], st_ref[...])
    y = (combine(w1_ref, 0, taps) * z).astype(BF)
    i, k = iota((WIN, WIN), 0), iota((WIN, WIN), 1)
    same = (k + base >= prior) == (i + base >= prior)
    taps = [y.astype(F32)] + [dot(one((k == i - o) & same), y) for o in (1, 2)]
    w = (combine(w2_ref, 1, taps) * combine(w2_ref, 2, taps)).astype(BF)
    head = y_ref[...]
    i, k = iota((16, WIN), 0), iota((16, WIN), 1) - WIN
    ih, kh = iota((16, 16), 0), iota((16, 16), 1)
    reach = (i < own) & ((prior >= length) | (k + length >= prior))
    far = [dot(one((k == i - o) & reach), y) for o in (1, 2)]
    near = [dot(shift_matrix(16, o, own), head) for o in (1, 2)]
    taps = (head.astype(F32), near[0] + far[0], near[1] + far[1])
    wh = combine(w2_ref, 1, taps) * combine(w2_ref, 2, taps)
    z = z_ref[...] + dot(b_ref[...], w) + dot(bh_ref[...], wh.astype(BF))
    q = q_ref[...]
    q = jnp.concatenate([combine(w2_ref, 0, taps), q[16:]], 0)
    out_ref[...] = (q * z).astype(BF)


def per_device(inputs, bounds, feat_first, li_decay, li_residue, feat_second, mr_filter):
    length, channels = inputs.shape
    groups, modes = li_decay.shape
    lanes = channels // groups
    filter_len = mr_filter.shape[1]
    rows = filter_len + 3 + (-(filter_len + 3)) % 16
    cut = length - rows + 2
    size = lax.axis_size("seq")
    place = lax.axis_index("seq")

    def behind(array, by):
        return lax.ppermute(array, "seq", [(i, i + by) for i in range(size - by)])

    own_row = jnp.broadcast_to(bounds.astype(BF)[:, None], (1, channels))
    edge = behind(jnp.concatenate([inputs[length - 2 :], own_row], 0), 1)
    tail = behind(inputs[length - rows :], 1)
    prior = jnp.where(place == 0, length, edge[2, 0].astype(F32).astype(jnp.int32))
    scal = jnp.stack([bounds[0], prior, (place % 2).astype(jnp.int32)])

    sm = pl.BlockSpec(memory_space=SMEM)
    whole = pl.BlockSpec(memory_space=pltpu.VMEM)
    params = pltpu.CompilerParams(vmem_limit_bytes=48 * 1024 * 1024)

    def block(*shape):
        return pl.BlockSpec(shape, lambda g: (0,) * (len(shape) - 1) + (g,))

    def table(*shape):
        return pl.BlockSpec((None,) + shape, lambda g: (g, 0, 0))

    def fixed(*shape):
        return pl.BlockSpec(shape, lambda g: (0,) * len(shape))

    shifts = pltpu.VMEM((2, length, length), BF)
    mine = pl.pallas_call(
        functools.partial(states_kernel, cut, modes),
        grid=(groups,),
        in_specs=[sm, block(length, lanes), block(3, lanes), block(3, 3, lanes), fixed(groups, modes)],
        out_specs=fixed(2 * modes, channels + LANE),
        out_shape=jax.ShapeDtypeStruct((2 * modes, channels + LANE), BF),
        scratch_shapes=[shifts],
        compiler_params=params,
        cost_estimate=pl.CostEstimate(flops=2 * 10**9, bytes_accessed=2**21, transcendentals=0),
        name="states",
    )(scal, inputs, edge, feat_first, li_decay)
    other = lax.ppermute(mine, "seq", [(i, i ^ 1) for i in range(size)])
    pair = pl.pallas_call(
        functools.partial(pair_kernel, cut, modes, length),
        in_specs=[sm] + [whole] * 3,
        out_specs=whole,
        out_shape=jax.ShapeDtypeStruct(mine.shape, BF),
        compiler_params=params,
        name="pair",
    )(scal, mine, other, li_decay)
    near = behind(pair, 2)
    far = [behind(pair[:modes], by) for by in range(4, size, 2)]
    state_shape = jax.ShapeDtypeStruct((3 * modes, channels), BF)
    own_state, win_state = pl.pallas_call(
        functools.partial(carry_kernel, cut, modes, length),
        in_specs=[sm] + [whole] * (3 + len(far)),
        out_specs=[whole] * 2,
        out_shape=[state_shape] * 2,
        compiler_params=params,
        name="carry",
    )(scal, other, near, li_decay, *far)

    shapes = [
        (length, length), (WIN, WIN), (length, 3 * modes), (WIN, 3 * modes),
        (length, length), (WIN, WIN), (WIN, 16),
    ]
    t_own, t_win, r_own, r_win, b_own, b_win, b_head = pl.pallas_call(
        functools.partial(tables_kernel, cut, modes, length),
        grid=(groups,),
        in_specs=[sm, fixed(groups, modes), fixed(groups, modes), table(1, filter_len)],
        out_specs=[table(*s) for s in shapes],
        out_shape=[jax.ShapeDtypeStruct((groups,) + s, BF) for s in shapes],
        compiler_params=params,
        cost_estimate=pl.CostEstimate(flops=8 * 10**9, bytes_accessed=2**22, transcendentals=0),
        name="tables",
    )(scal, li_decay, li_residue, mr_filter.reshape(groups, 1, filter_len))

    out_shape = jax.ShapeDtypeStruct((length, channels), BF)
    head_shape = jax.ShapeDtypeStruct((WIN, channels), F32)
    out, z_head, q_head, y_head = pl.pallas_call(
        own_kernel,
        grid=(groups,),
        in_specs=[
            sm, block(length, lanes), block(3, lanes), block(3, 3, lanes), block(3, 3, lanes),
            table(length, length), table(length, 3 * modes), table(length, length),
            block(3 * modes, lanes),
        ],
        out_specs=[block(length, lanes), block(WIN, lanes), block(WIN, lanes), block(16, lanes)],
        out_shape=[out_shape, head_shape, head_shape, jax.ShapeDtypeStruct((16, channels), BF)],
        scratch_shapes=[shifts],
        compiler_params=params,
        cost_estimate=pl.CostEstimate(flops=8 * 10**9, bytes_accessed=2**23, transcendentals=0),
        name="own",
    )(scal, inputs, edge, feat_first, feat_second, t_own, r_own, b_own, own_state)
    return pl.pallas_call(
        functools.partial(head_kernel, length=length),
        grid=(groups,),
        in_specs=[
            sm, block(rows, lanes), block(3, 3, lanes), block(3, 3, lanes),
            table(WIN, WIN), table(WIN, 3 * modes), table(WIN, WIN), table(WIN, 16),
            block(3 * modes, lanes), block(WIN, lanes), block(WIN, lanes), block(16, lanes),
            pl.BlockSpec(memory_space=pl.ANY),
        ],
        out_specs=block(WIN, lanes),
        out_shape=out_shape,
        input_output_aliases={12: 0},
        compiler_params=params,
        cost_estimate=pl.CostEstimate(flops=8 * 10**9, bytes_accessed=2**22, transcendentals=0),
        name="head",
    )(
        scal, tail, feat_first, feat_second, t_win, r_win, b_win, b_head, win_state,
        z_head, q_head, y_head, out,
    )


def solution(mesh):
    in_specs = (
        P(("groups", "seq"), "chan"),
        P(("groups", "seq")),
        P(None, None, "chan"),
        P("chan", None),
        P("chan", None),
        P(None, None, "chan"),
        P("chan", None),
    )
    out_specs = P(("groups", "seq"), "chan")
    return jax.shard_map(
        per_device, mesh=mesh, in_specs=in_specs, out_specs=out_specs, check_vma=False
    )
```

```python
import functools
import math

import jax
import jax.numpy as jnp
from jax import lax
from jax.experimental import pallas as pl
from jax.experimental.pallas import tpu as pltpu
from jax.sharding import PartitionSpec as P

F32 = jnp.float32
BF = jnp.bfloat16
WIN = 144
LANE = 128
SMEM = pltpu.SMEM


def dot(a, b):
    return lax.dot_general(a, b, (((1,), (0,)), ((), ())), preferred_element_type=F32)


def iota(shape, dim):
    return lax.broadcasted_iota(jnp.int32, shape, dim)


def column(row):
    n = row.shape[1]
    return jnp.sum(
        jnp.where(iota((n, n), 0) == iota((n, n), 1), row, 0.0), axis=1, keepdims=True
    )


def one(cond):
    return jnp.where(cond, 1.0, 0.0).astype(BF)


def combine(w, branch, taps, cols):
    total = w[branch, 0:1, cols] * taps[0]
    for o in (1, 2):
        total = total + w[branch, o : o + 1, cols] * taps[o]
    return total


def spans(count, lanes):
    return [(i, slice(i * lanes, (i + 1) * lanes)) for i in range(count)]


def write_masks(ref, offset, own, prior, length):
    rows = ref.shape[1]
    t = iota((rows, LANE), 0) - offset
    before = jnp.where(prior < length, prior, -length) - length
    one_back = (t != own) & (t != before)
    two_back = one_back & (t - 1 != own) & (t - 1 != before)
    ref[0] = jnp.where(one_back, 1.0, 0.0)
    ref[1] = jnp.where(two_back, 1.0, 0.0)


def widen(mask, lanes):
    return jnp.concatenate([mask] * (lanes // LANE), 1)


def first_taps(x, edge, mask_ref):
    length, lanes = x.shape
    x0 = x.astype(F32)
    row = iota((8, lanes), 0)
    e0, e1 = edge[0:1].astype(F32), edge[1:2].astype(F32)
    x1, x2 = pltpu.roll(x0, 1, 0), pltpu.roll(x0, 2, 0)
    top1 = jnp.where(row == 0, e1, x1[:8])
    top2 = jnp.where(row == 0, e0, jnp.where(row == 1, e1, x2[:8]))
    x1 = jnp.concatenate([top1, x1[8:]], 0) * widen(mask_ref[0], lanes)
    x2 = jnp.concatenate([top2, x2[8:]], 0) * widen(mask_ref[1], lanes)
    return x0, x1, x2


def split(v):
    hi = v.astype(BF)
    return hi, (v - hi.astype(F32)).astype(BF)


def states_kernel(
    cut, modes, lanes, scal, x_ref, edge_ref, w_ref, dec_ref, out_ref, part_ref, mask_ref
):
    step = pl.program_id(0)
    length, step_lanes = x_ref.shape
    count = step_lanes // lanes
    own, prior = scal[0], scal[1]

    @pl.when(step == 0)
    def _():
        write_masks(mask_ref, 0, own, prior, length)
        flag = jnp.full((modes, LANE), own, jnp.int32).astype(F32)
        out_ref[:, pl.ds(out_ref.shape[1] - LANE, LANE)] = flag.astype(BF)

    p = iota((modes, length), 1)
    lag = (length - 1 - p).astype(F32)
    lag_cut = jnp.maximum(cut - 1 - p, 0).astype(F32)
    reach = (p >= own) | (own >= length)
    reach_cut = (p < cut) & ((p >= own) | (own >= cut))
    for i, cols in spans(count, lanes):
        taps = first_taps(x_ref[:, cols], edge_ref[:, cols], mask_ref)
        u = (combine(w_ref, 1, taps, cols) * combine(w_ref, 2, taps, cols)).astype(BF)
        dec = column(dec_ref[pl.ds(step * count + i, 1), :])
        full = jnp.where(reach, jnp.exp(-dec * lag), 0.0)
        part = jnp.where(reach_cut, jnp.exp(-dec * lag_cut), 0.0)
        hi, lo = split(jnp.concatenate([full, part], 0))
        both = dot(jnp.concatenate([hi, lo], 0), u)
        state = both[: 2 * modes] + both[2 * modes :]
        at = pl.ds(pl.multiple_of((step * count + i) * lanes, lanes), lanes)
        out_ref[:, at] = state[:modes].astype(BF)
        part_ref[:, at] = state[modes:].astype(BF)


def pair_kernel(modes, length, scal, mine_ref, other_ref, dec_ref, out_ref):
    groups = dec_ref.shape[0]
    width = mine_ref.shape[1] - LANE
    lanes = width // groups
    even = scal[2] == 0
    end = slice(width, width + LANE)

    def pick(cols):
        a, b = mine_ref[:, cols].astype(F32), other_ref[:, cols].astype(F32)
        return jnp.where(even, a, b), jnp.where(even, b, a)

    top, low = slice(0, modes), slice(modes, 2 * modes)
    f_bound, s_bound = pick(end)
    free_f = jnp.where(f_bound >= length, 1.0, 0.0)
    free_s = jnp.where(s_bound >= length, 1.0, 0.0)
    out_ref[top, end] = (free_f * free_s).astype(BF)
    out_ref[low, end] = free_f.astype(BF)
    for g in range(groups):
        cols = slice(g * lanes, (g + 1) * lanes)
        dec = column(dec_ref[g : g + 1, :])
        first, second = pick(cols)
        out_ref[top, cols] = (second + jnp.exp(-dec * length) * free_s[:, :1] * first).astype(BF)
        out_ref[low, cols] = first.astype(BF)


def carry_kernel(modes, length, near_ref, dec_ref, *refs):
    far, (send_ref, own_ref, late_ref) = refs[:-3], refs[-3:]
    groups = dec_ref.shape[0]
    width = own_ref.shape[1]
    lanes = width // groups
    top, low = slice(0, modes), slice(modes, 2 * modes)
    near_free = near_ref[top, width : width + LANE].astype(F32)[:, :1]
    late_free = near_ref[low, width : width + LANE].astype(F32)[:, :1]
    far_free = [f[:, width : width + LANE].astype(F32)[:, :1] for f in far]
    for g in range(groups):
        cols = slice(g * lanes, (g + 1) * lanes)
        dec = column(dec_ref[g : g + 1, :])
        once = jnp.exp(-dec * length)
        pair = jnp.exp(-dec * (2 * length))
        behind = jnp.zeros((modes, lanes), F32)
        for f, free in zip(far[::-1], far_free[::-1]):
            behind = f[:, cols].astype(F32) + pair * free * behind
        whole = near_ref[top, cols].astype(F32) + pair * near_free * behind
        send_ref[:, cols] = whole.astype(BF)
        own_ref[:, cols] = whole
        late_ref[:, cols] = near_ref[low, cols].astype(F32) + once * late_free * behind


def place_kernel(
    cut, modes, length, scal, other_ref, part_ref, sent_ref, even_own, even_late, dec_ref,
    own_ref, win_ref,
):
    groups = dec_ref.shape[0]
    lanes = own_ref.shape[1] // groups
    even = scal[2] == 0
    prior = scal[1]
    pass_own = jnp.where(prior >= length, 1.0, 0.0)
    pass_cut = jnp.where(prior >= cut, 1.0, 0.0)
    for g in range(groups):
        cols = slice(g * lanes, (g + 1) * lanes)
        dec = column(dec_ref[g : g + 1, :])
        sent = sent_ref[:, cols].astype(F32)
        odd_own = other_ref[:, cols].astype(F32) + jnp.exp(-dec * length) * pass_own * sent
        before = jnp.where(even, even_late[:, cols], sent)
        own = jnp.where(even, even_own[:, cols], odd_own)
        win = part_ref[:, cols].astype(F32) + jnp.exp(-dec * cut) * pass_cut * before
        for ref, v in ((own_ref, own), (win_ref, win)):
            hi, lo = split(v)
            ref[:, cols] = jnp.concatenate([hi, lo, hi], 0)


def tables_kernel(cut, modes, length, scal, dec_ref, res_ref, mr_ref, *outs):
    t_own, t_own_lo, t_win, t_win_lo, r_own, r_win, b_win, b_own = outs
    g = pl.program_id(0)
    own, prior = scal[0], scal[1]
    wide = 2 * length
    base = length - WIN
    dec_row = dec_ref[pl.ds(g, 1), :]
    weight_row = res_ref[pl.ds(g, 1), :] * jnp.sqrt(
        jnp.maximum(1.0 - jnp.exp(-2.0 * dec_row), 0.0)
    ) / math.sqrt(modes)
    small = 2.0 * dec_row
    series = small * (1.0 - small * (0.5 - small * (1.0 / 6 - small * (1.0 / 24))))
    weight_row = jnp.where(
        small < 0.05,
        res_ref[pl.ds(g, 1), :] * jnp.sqrt(series) / math.sqrt(modes),
        weight_row,
    )
    dec, weight = column(dec_row), column(weight_row)
    back = iota((modes, wide), 1)
    back = jnp.where(back == 0, 0, wide - back).astype(F32)
    taps = jnp.sum(weight * jnp.exp(-dec * back), axis=0, keepdims=True)
    full = pltpu.roll(jnp.broadcast_to(taps, (length, wide)), 0, 1, stride=1, stride_axis=0)
    t, p = iota((length, length), 0), iota((length, length), 1)
    seen = (p <= t) & ((p >= own) == (t >= own))
    t_own[...], t_own_lo[...] = split(jnp.where(seen, full[:, :length], 0.0))
    tw, pw = iota((WIN, WIN), 0) + base, iota((WIN, WIN), 1) + base
    seen = (pw <= tw) & (pw >= cut) & ((pw >= prior) == (tw >= prior))
    t_win[...], t_win_lo[...] = split(jnp.where(seen, full[:WIN, :WIN], 0.0))

    tl = iota((modes, length), 1)
    rise = jnp.where(tl < own, weight * jnp.exp(-dec * (tl + 1).astype(F32)), 0.0)
    wl = tl + base
    lag = jnp.maximum(wl - cut + 1, 0)
    fits = (wl >= cut) & ((prior < cut) | (prior > wl))
    rise_w = jnp.where(fits, weight * jnp.exp(-dec * lag.astype(F32)), 0.0)
    for ref, v, rows in ((r_own, rise, length), (r_win, rise_w, WIN)):
        hi = v.astype(BF).astype(F32)
        stack = jnp.concatenate([hi, hi, v - hi, jnp.zeros((LANE - 3 * modes, length), F32)], 0)
        ref[...] = jnp.transpose(stack)[:rows, : 3 * modes].astype(BF)

    count = mr_ref.shape[1]
    o, n = iota((count, wide), 0), iota((count, wide), 1)
    back = dot(mr_ref[...], one(((n == 0) & (o == 0)) | ((n > 0) & (wide - n == o))))
    band = pltpu.roll(
        jnp.broadcast_to(back, (WIN + length, wide)), 0, 1, stride=1, stride_axis=0
    )
    seen = (p <= t) & ((p >= own) == (t >= own))
    b_own[...] = jnp.where(seen, band[:length, :length], 0.0).astype(BF)
    tb, pb = iota((length, WIN), 0), iota((length, WIN), 1) + base
    seen = (tb < own) & ((prior >= length) | (pb >= prior))
    b_win[...] = jnp.where(seen, band[WIN : WIN + length, :WIN], 0.0).astype(BF)


def near_kernel(lanes, scal, x_ref, edge_ref, w_ref, t_ref, lo_ref, q_ref, z_ref, mask_ref):
    @pl.when(pl.program_id(0) == 0)
    def _():
        write_masks(mask_ref, 0, scal[0], scal[1], x_ref.shape[0])

    for i, cols in spans(x_ref.shape[1] // lanes, lanes):
        taps = first_taps(x_ref[:, cols], edge_ref[:, cols], mask_ref)
        u = (combine(w_ref, 1, taps, cols) * combine(w_ref, 2, taps, cols)).astype(BF)
        z_ref[:, cols] = dot(t_ref[i], u) + dot(lo_ref[i], u)
        q_ref[:, cols] = combine(w_ref, 0, taps, cols)


def near_tail_kernel(length, lanes, scal, tail_ref, w_ref, t_ref, lo_ref, q_ref, z_ref, sh_ref):
    rows = tail_ref.shape[0]
    prior = scal[1]

    @pl.when(pl.program_id(0) == 0)
    def _():
        tb = iota((WIN, rows), 0) + (length - WIN)
        pb = iota((WIN, rows), 1) + (length - rows)
        for o in range(3):
            sh_ref[o] = one((pb == tb - o) & ((pb >= prior) == (tb >= prior)))

    for i, cols in spans(tail_ref.shape[1] // lanes, lanes):
        x = tail_ref[:, cols]
        taps = [dot(sh_ref[o], x) for o in range(3)]
        u = (combine(w_ref, 1, taps, cols) * combine(w_ref, 2, taps, cols)).astype(BF)
        z_ref[:, cols] = dot(t_ref[i], u) + dot(lo_ref[i], u)
        q_ref[:, cols] = combine(w_ref, 0, taps, cols)


def final_kernel(
    lanes, scal, q_ref, z_ref, qt_ref, zt_ref, r_ref, rt_ref, st_ref, stt_ref, w_ref, bt_ref,
    b_ref, out_ref, mask_ref,
):
    length = q_ref.shape[0]

    @pl.when(pl.program_id(0) == 0)
    def _():
        write_masks(mask_ref, WIN, scal[0], scal[1], length)

    for i, cols in spans(q_ref.shape[1] // lanes, lanes):
        yt = qt_ref[:, cols] * (zt_ref[:, cols] + dot(rt_ref[i], stt_ref[:, cols]))
        y = q_ref[:, cols] * (z_ref[:, cols] + dot(r_ref[i], st_ref[:, cols]))
        y = jnp.concatenate([yt, y], 0).astype(BF).astype(F32)
        m1, m2 = widen(mask_ref[0], lanes), widen(mask_ref[1], lanes)
        taps = (y, pltpu.roll(y, 1, 0) * m1, pltpu.roll(y, 2, 0) * m2)
        w = (combine(w_ref, 1, taps, cols) * combine(w_ref, 2, taps, cols)).astype(BF)
        z = dot(bt_ref[i], w[:WIN]) + dot(b_ref[i], w[WIN:])
        q = combine(w_ref, 0, [a[WIN:] for a in taps], cols)
        out_ref[:, cols] = (q * z).astype(BF)


def per_device(inputs, bounds, feat_first, li_decay, li_residue, feat_second, mr_filter):
    length, channels = inputs.shape
    groups, modes = li_decay.shape
    lanes = channels // groups
    filter_len = mr_filter.shape[1]
    rows = filter_len + 3
    cut = length - rows + 2
    size = lax.axis_size("seq")
    place = lax.axis_index("seq")

    def behind(array, by):
        return lax.ppermute(array, "seq", [(i, i + by) for i in range(size - by)])

    own_row = jnp.broadcast_to(bounds.astype(BF)[:, None], (1, channels))
    edge = behind(jnp.concatenate([inputs[length - 2 :], own_row], 0), 1)
    prior = jnp.where(place == 0, length, edge[2, 0].astype(F32).astype(jnp.int32))
    scal = jnp.stack([bounds[0], prior, (place % 2).astype(jnp.int32)])

    sm = pl.BlockSpec(memory_space=SMEM)
    whole = pl.BlockSpec(memory_space=pltpu.VMEM)
    params = pltpu.CompilerParams(vmem_limit_bytes=24 * 1024 * 1024)
    count = 2 if groups % 2 == 0 else 1
    steps, wide = groups // count, lanes * count

    def block(*shape):
        return pl.BlockSpec(shape, lambda g: (0,) * (len(shape) - 1) + (g,))

    def table(*shape):
        return pl.BlockSpec((count,) + shape, lambda g: (g, 0, 0))

    def single(*shape):
        return pl.BlockSpec((None,) + shape, lambda g: (g, 0, 0))

    def fixed(*shape):
        return pl.BlockSpec(shape, lambda g: (0,) * len(shape))

    mine, part = pl.pallas_call(
        functools.partial(states_kernel, cut, modes, lanes),
        grid=(steps,),
        in_specs=[sm, block(length, wide), block(3, wide), block(3, 3, wide), fixed(groups, modes)],
        out_specs=[fixed(modes, channels + LANE), fixed(modes, channels)],
        out_shape=[
            jax.ShapeDtypeStruct((modes, channels + LANE), BF),
            jax.ShapeDtypeStruct((modes, channels), BF),
        ],
        scratch_shapes=[pltpu.VMEM((2, length, LANE), F32)],
        compiler_params=params,
        cost_estimate=pl.CostEstimate(flops=2 * 10**9, bytes_accessed=2**21, transcendentals=0),
        name="states",
    )(scal, inputs, edge, feat_first, li_decay)
    other = lax.ppermute(mine, "seq", [(i, i ^ 1) for i in range(size)])
    inputs_late, other = lax.optimization_barrier((inputs, other))
    tail_rows, other = lax.optimization_barrier((inputs_late[length - rows :], other))
    tail = behind(tail_rows, 1)
    pair = pl.pallas_call(
        functools.partial(pair_kernel, modes, length),
        in_specs=[sm] + [whole] * 3,
        out_specs=whole,
        out_shape=jax.ShapeDtypeStruct((2 * modes, channels + LANE), BF),
        compiler_params=params,
        name="pair",
    )(scal, mine, other, li_decay)
    near = lax.ppermute(pair, "seq", [(i, i + 2) for i in range(0, size - 2, 2)])
    far = [
        lax.ppermute(pair[:modes], "seq", [(i, i + by) for i in range(0, size - by, 2)])
        for by in range(4, size, 2)
    ]
    state_shape = jax.ShapeDtypeStruct((modes, channels), F32)
    send, even_own, even_late = pl.pallas_call(
        functools.partial(carry_kernel, modes, length),
        in_specs=[whole] * (2 + len(far)),
        out_specs=[whole] * 3,
        out_shape=[jax.ShapeDtypeStruct((modes, channels), BF), state_shape, state_shape],
        compiler_params=params,
        name="carry",
    )(near, li_decay, *far)
    part, send = lax.optimization_barrier((part, send))
    part = behind(part, 1)
    sent = lax.ppermute(send, "seq", [(i, i + 1) for i in range(0, size, 2)])
    own_state, win_state = pl.pallas_call(
        functools.partial(place_kernel, cut, modes, length),
        in_specs=[sm] + [whole] * 6,
        out_specs=[whole] * 2,
        out_shape=[jax.ShapeDtypeStruct((3 * modes, channels), BF)] * 2,
        compiler_params=params,
        name="place",
    )(scal, other, part, sent, even_own, even_late, li_decay)

    shapes = [
        (length, length), (length, length), (WIN, WIN), (WIN, WIN),
        (length, 3 * modes), (WIN, 3 * modes), (length, WIN), (length, length),
    ]
    t_own, t_own_lo, t_win, t_win_lo, r_own, r_win, b_win, b_own = pl.pallas_call(
        functools.partial(tables_kernel, cut, modes, length),
        grid=(groups,),
        in_specs=[sm, fixed(groups, modes), fixed(groups, modes), single(1, filter_len)],
        out_specs=[single(*s) for s in shapes],
        out_shape=[jax.ShapeDtypeStruct((groups,) + s, BF) for s in shapes],
        compiler_params=params,
        cost_estimate=pl.CostEstimate(flops=8 * 10**9, bytes_accessed=2**22, transcendentals=0),
        name="tables",
    )(scal, li_decay, li_residue, mr_filter.reshape(groups, 1, filter_len))

    q_own, z_own = pl.pallas_call(
        functools.partial(near_kernel, lanes),
        grid=(steps,),
        in_specs=[
            sm, block(length, wide), block(3, wide), block(3, 3, wide),
            table(length, length), table(length, length),
        ],
        out_specs=[block(length, wide)] * 2,
        out_shape=[jax.ShapeDtypeStruct((length, channels), F32)] * 2,
        scratch_shapes=[pltpu.VMEM((2, length, LANE), F32)],
        compiler_params=params,
        cost_estimate=pl.CostEstimate(flops=8 * 10**9, bytes_accessed=2**23, transcendentals=0),
        name="near",
    )(scal, inputs, edge, feat_first, t_own, t_own_lo)
    q_win, z_win = pl.pallas_call(
        functools.partial(near_tail_kernel, length, lanes),
        grid=(steps,),
        in_specs=[
            sm, block(rows, wide), block(3, 3, wide), table(WIN, WIN), table(WIN, WIN),
        ],
        out_specs=[block(WIN, wide)] * 2,
        out_shape=[jax.ShapeDtypeStruct((WIN, channels), F32)] * 2,
        scratch_shapes=[pltpu.VMEM((3, WIN, rows), BF)],
        compiler_params=params,
        cost_estimate=pl.CostEstimate(flops=4 * 10**9, bytes_accessed=2**22, transcendentals=0),
        name="near_tail",
    )(scal, tail, feat_first, t_win, t_win_lo)
    return pl.pallas_call(
        functools.partial(final_kernel, lanes),
        grid=(steps,),
        in_specs=[
            sm, block(length, wide), block(length, wide), block(WIN, wide), block(WIN, wide),
            table(length, 3 * modes), table(WIN, 3 * modes),
            block(3 * modes, wide), block(3 * modes, wide), block(3, 3, wide),
            table(length, WIN), table(length, length),
        ],
        out_specs=block(length, wide),
        out_shape=jax.ShapeDtypeStruct((length, channels), BF),
        scratch_shapes=[pltpu.VMEM((2, WIN + length, LANE), F32)],
        compiler_params=params,
        cost_estimate=pl.CostEstimate(flops=8 * 10**9, bytes_accessed=2**24, transcendentals=0),
        name="final",
    )(
        scal, q_own, z_own, q_win, z_win, r_own, r_win, own_state, win_state, feat_second,
        b_win, b_own,
    )


def solution(mesh):
    in_specs = (
        P(("groups", "seq"), "chan"),
        P(("groups", "seq")),
        P(None, None, "chan"),
        P("chan", None),
        P("chan", None),
        P(None, None, "chan"),
        P("chan", None),
    )
    out_specs = P(("groups", "seq"), "chan")
    return jax.shard_map(
        per_device, mesh=mesh, in_specs=in_specs, out_specs=out_specs, check_vma=False
    )
```

```python
import functools
import math

import jax
import jax.numpy as jnp
from jax import lax
from jax.experimental import pallas as pl
from jax.experimental.pallas import tpu as pltpu
from jax.sharding import PartitionSpec as P

F32 = jnp.float32
BF = jnp.bfloat16
WIN = 144
LANE = 128
CHUNK = 32
SMEM = pltpu.SMEM


def dot(a, b):
    return lax.dot_general(a, b, (((1,), (0,)), ((), ())), preferred_element_type=F32)


def iota(shape, dim):
    return lax.broadcasted_iota(jnp.int32, shape, dim)


def column(row):
    n = row.shape[1]
    return jnp.sum(
        jnp.where(iota((n, n), 0) == iota((n, n), 1), row, 0.0), axis=1, keepdims=True
    )


def one(cond):
    return jnp.where(cond, 1.0, 0.0).astype(BF)


def weights_of(w_ref, cols):
    return [[w_ref[b, o : o + 1, cols] for o in range(3)] for b in range(3)]


def combine(w, taps):
    return w[0] * taps[0] + w[1] * taps[1] + w[2] * taps[2]


def taps_at(ref, mask_ref, at, cols):
    rows = ref[at.start : at.stop + 8, cols]
    return (
        rows[8:],
        pltpu.roll(rows, 1, 0)[8:] * mask_ref[0, at, :],
        pltpu.roll(rows, 2, 0)[8:] * mask_ref[1, at, :],
    )


def chunks(first, last, rows=CHUNK):
    return [slice(r, min(r + rows, last)) for r in range(first, last, rows)]


def tiles(lanes):
    return [slice(c, c + LANE) for c in range(0, lanes, LANE)]


def spans(count, lanes):
    return [(i, slice(i * lanes, (i + 1) * lanes)) for i in range(count)]


def write_masks(ref, offset, own, prior, length):
    rows = ref.shape[1]
    t = iota((rows, LANE), 0) - offset
    before = jnp.where(prior < length, prior, -length) - length
    one_back = (t != own) & (t != before)
    two_back = one_back & (t - 1 != own) & (t - 1 != before)
    ref[0] = jnp.where(one_back, 1.0, 0.0)
    ref[1] = jnp.where(two_back, 1.0, 0.0)


def split(v):
    hi = v.astype(BF)
    return hi, (v - hi.astype(F32)).astype(BF)


def states_kernel(
    cut, modes, lanes, scal, x_ref, edge_ref, w_ref, dec_ref, out_ref, part_ref, q_ref, u_ref,
    mask_ref, x_scr,
):
    length, width = x_ref.shape
    own, prior = scal[0], scal[1]
    write_masks(mask_ref, 0, own, prior, length)
    flag = jnp.full((modes, LANE), own, jnp.int32).astype(F32)
    out_ref[:, width:] = flag.astype(BF)

    p = iota((modes, length), 1)
    lag = (length - 1 - p).astype(F32)
    lag_cut = jnp.maximum(cut - 1 - p, 0).astype(F32)
    reach = (p >= own) | (own >= length)
    reach_cut = (p < cut) & ((p >= own) | (own >= cut))
    for i, cols in spans(width // lanes, lanes):
        scr = x_scr.at[i % x_scr.shape[0]]
        scr[6:8, :] = edge_ref[:, cols].astype(F32)[:2]
        scr[8 : 8 + length, :] = x_ref[:, cols].astype(F32)
        for tile in tiles(lanes):
            here = slice(cols.start + tile.start, cols.start + tile.stop)
            w = weights_of(w_ref, here)
            for at in chunks(0, length):
                taps = taps_at(scr, mask_ref, at, tile)
                u_ref[at, here] = (combine(w[1], taps) * combine(w[2], taps)).astype(BF)
                q_ref[at, here] = combine(w[0], taps)
        dec = column(dec_ref[i : i + 1, :])
        full = jnp.where(reach, jnp.exp(-dec * lag), 0.0)
        part = jnp.where(reach_cut, jnp.exp(-dec * lag_cut), 0.0)
        hi, lo = split(jnp.concatenate([full, part], 0))
        both = dot(jnp.concatenate([hi, lo], 0), u_ref[:, cols])
        state = both[: 2 * modes] + both[2 * modes :]
        out_ref[:, cols] = state[:modes].astype(BF)
        part_ref[:, cols] = state[modes:].astype(BF)


def pair_kernel(modes, length, scal, mine_ref, other_ref, dec_ref, out_ref):
    groups = dec_ref.shape[0]
    width = mine_ref.shape[1] - LANE
    lanes = width // groups
    even = scal[2] == 0
    end = slice(width, width + LANE)

    def pick(cols):
        a, b = mine_ref[:, cols].astype(F32), other_ref[:, cols].astype(F32)
        return jnp.where(even, a, b), jnp.where(even, b, a)

    top, low = slice(0, modes), slice(modes, 2 * modes)
    f_bound, s_bound = pick(end)
    free_f = jnp.where(f_bound >= length, 1.0, 0.0)
    free_s = jnp.where(s_bound >= length, 1.0, 0.0)
    out_ref[top, end] = (free_f * free_s).astype(BF)
    out_ref[low, end] = free_f.astype(BF)
    for g in range(groups):
        cols = slice(g * lanes, (g + 1) * lanes)
        dec = column(dec_ref[g : g + 1, :])
        first, second = pick(cols)
        out_ref[top, cols] = (second + jnp.exp(-dec * length) * free_s[:, :1] * first).astype(BF)
        out_ref[low, cols] = first.astype(BF)


def carry_kernel(modes, length, near_ref, dec_ref, *refs):
    far, (send_ref, own_ref, late_ref) = refs[:-3], refs[-3:]
    groups = dec_ref.shape[0]
    width = own_ref.shape[1]
    lanes = width // groups
    top, low = slice(0, modes), slice(modes, 2 * modes)
    near_free = near_ref[top, width : width + LANE].astype(F32)[:, :1]
    late_free = near_ref[low, width : width + LANE].astype(F32)[:, :1]
    far_free = [f[:, width : width + LANE].astype(F32)[:, :1] for f in far]
    for g in range(groups):
        cols = slice(g * lanes, (g + 1) * lanes)
        dec = column(dec_ref[g : g + 1, :])
        once = jnp.exp(-dec * length)
        pair = jnp.exp(-dec * (2 * length))
        behind = jnp.zeros((modes, lanes), F32)
        for f, free in zip(far[::-1], far_free[::-1]):
            behind = f[:, cols].astype(F32) + pair * free * behind
        whole = near_ref[top, cols].astype(F32) + pair * near_free * behind
        send_ref[:, cols] = whole.astype(BF)
        own_ref[:, cols] = whole
        late_ref[:, cols] = near_ref[low, cols].astype(F32) + once * late_free * behind


def place_kernel(
    cut, modes, length, scal, other_ref, part_ref, sent_ref, even_own, even_late, dec_ref,
    own_ref, win_ref,
):
    groups = dec_ref.shape[0]
    lanes = own_ref.shape[1] // groups
    even = scal[2] == 0
    prior = scal[1]
    pass_own = jnp.where(prior >= length, 1.0, 0.0)
    pass_cut = jnp.where(prior >= cut, 1.0, 0.0)
    for g in range(groups):
        cols = slice(g * lanes, (g + 1) * lanes)
        dec = column(dec_ref[g : g + 1, :])
        sent = sent_ref[:, cols].astype(F32)
        odd_own = other_ref[:, cols].astype(F32) + jnp.exp(-dec * length) * pass_own * sent
        before = jnp.where(even, even_late[:, cols], sent)
        own = jnp.where(even, even_own[:, cols], odd_own)
        win = part_ref[: dec_ref.shape[1], cols].astype(F32) + jnp.exp(-dec * cut) * pass_cut * before
        for ref, v in ((own_ref, own), (win_ref, win)):
            hi, lo = split(v)
            ref[:, cols] = jnp.concatenate([hi, lo, hi], 0)


def tables_kernel(cut, modes, length, scal, dec_ref, res_ref, mr_ref, *outs):
    t_own, t_win, r_own, r_win, b_win, b_own = outs
    g = pl.program_id(0)
    own, prior = scal[0], scal[1]
    wide = 2 * length
    base = length - WIN
    dec_row = dec_ref[pl.ds(g, 1), :]
    weight_row = res_ref[pl.ds(g, 1), :] * jnp.sqrt(
        jnp.maximum(1.0 - jnp.exp(-2.0 * dec_row), 0.0)
    ) / math.sqrt(modes)
    small = 2.0 * dec_row
    series = small * (1.0 - small * (0.5 - small * (1.0 / 6 - small * (1.0 / 24))))
    weight_row = jnp.where(
        small < 0.05,
        res_ref[pl.ds(g, 1), :] * jnp.sqrt(series) / math.sqrt(modes),
        weight_row,
    )
    dec, weight = column(dec_row), column(weight_row)
    back = iota((modes, wide), 1)
    back = jnp.where(back == 0, 0, wide - back).astype(F32)
    taps = jnp.sum(weight * jnp.exp(-dec * back), axis=0, keepdims=True)
    full = pltpu.roll(jnp.broadcast_to(taps, (length, wide)), 0, 1, stride=1, stride_axis=0)
    t, p = iota((length, length), 0), iota((length, length), 1)
    seen = (p <= t) & ((p >= own) == (t >= own))
    t_own[:length, :], t_own[length:, :] = split(jnp.where(seen, full[:, :length], 0.0))
    tw, pw = iota((WIN, WIN), 0) + base, iota((WIN, WIN), 1) + base
    seen = (pw <= tw) & (pw >= cut) & ((pw >= prior) == (tw >= prior))
    t_win[:WIN, :], t_win[WIN:, :] = split(jnp.where(seen, full[:WIN, :WIN], 0.0))

    tl = iota((modes, length), 1)
    rise = jnp.where(tl < own, weight * jnp.exp(-dec * (tl + 1).astype(F32)), 0.0)
    wl = tl + base
    lag = jnp.maximum(wl - cut + 1, 0)
    fits = (wl >= cut) & ((prior < cut) | (prior > wl))
    rise_w = jnp.where(fits, weight * jnp.exp(-dec * lag.astype(F32)), 0.0)
    for ref, v, rows in ((r_own, rise, length), (r_win, rise_w, WIN)):
        hi = v.astype(BF).astype(F32)
        stack = jnp.concatenate([hi, hi, v - hi, jnp.zeros((LANE - 3 * modes, length), F32)], 0)
        ref[...] = jnp.transpose(stack)[:rows, : 3 * modes].astype(BF)

    count = mr_ref.shape[1]
    o, n = iota((count, wide), 0), iota((count, wide), 1)
    back = dot(mr_ref[...], one(((n == 0) & (o == 0)) | ((n > 0) & (wide - n == o))))
    band = pltpu.roll(
        jnp.broadcast_to(back, (WIN + length, wide)), 0, 1, stride=1, stride_axis=0
    )
    seen = (p <= t) & ((p >= own) == (t >= own))
    b_own[...] = jnp.where(seen, band[:length, :length], 0.0).astype(BF)
    tb, pb = iota((length, WIN), 0), iota((length, WIN), 1) + base
    seen = (tb < own) & ((prior >= length) | (pb >= prior))
    b_win[...] = jnp.where(seen, band[WIN : WIN + length, :WIN], 0.0).astype(BF)


def tail_kernel(
    modes, length, lanes, scal, tail_ref, w_ref, q_ref, u_ref, mask_ref, x_scr
):
    rows = tail_ref.shape[0] - modes

    write_masks(mask_ref, WIN, scal[0], scal[1], length)
    x_scr[:, : 8 + WIN - rows, :] = jnp.zeros(
        (x_scr.shape[0], 8 + WIN - rows, x_scr.shape[2]), F32
    )

    for i, cols in spans(tail_ref.shape[1] // lanes, lanes):
        scr = x_scr.at[i]
        scr[8 + WIN - rows : 8 + WIN, :] = tail_ref[modes:, cols].astype(F32)
        for tile in tiles(lanes):
            here = slice(cols.start + tile.start, cols.start + tile.stop)
            w = weights_of(w_ref, here)
            for at in chunks(0, WIN):
                taps = taps_at(scr, mask_ref, at, tile)
                u_ref[at, here] = (combine(w[1], taps) * combine(w[2], taps)).astype(BF)
                q_ref[at, here] = combine(w[0], taps)


def final_kernel(
    lanes, scal, q_ref, u_ref, qt_ref, ut_ref, t_ref, tt_ref, r_ref, rt_ref, st_ref, stt_ref,
    w_ref, bt_ref, b_ref, out_ref, mask_ref, y_scr, w_scr, q_scr, z_scr, o_scr, sems,
):
    length = q_ref.shape[0]

    write_masks(mask_ref, WIN, scal[0], scal[1], length)
    y_scr[:, :8, :] = jnp.zeros((y_scr.shape[0], 8, y_scr.shape[2]), F32)
    copies = []
    for i, cols in spans(q_ref.shape[1] // lanes, lanes):
        k = i % y_scr.shape[0]
        ys, ws, qs, zs = y_scr.at[k], w_scr.at[k], q_scr.at[k], z_scr.at[k]
        near = dot(tt_ref[i], ut_ref[:, cols])
        zs[:WIN, :] = near[:WIN] + near[WIN:] + dot(rt_ref[i], stt_ref[:, cols])
        near = dot(t_ref[i], u_ref[:, cols])
        zs[WIN:, :] = near[:length] + near[length:] + dot(r_ref[i], st_ref[:, cols])
        for tile in tiles(lanes):
            here = slice(cols.start + tile.start, cols.start + tile.stop)
            for at in chunks(0, WIN) + chunks(WIN, WIN + length):
                if at.start < WIN:
                    q = qt_ref[at, here]
                else:
                    q = q_ref[at.start - WIN : at.stop - WIN, here]
                y = (q * zs[at, tile]).astype(BF).astype(F32)
                ys[8 + at.start : 8 + at.stop, tile] = y
            w = weights_of(w_ref, here)
            for at in chunks(0, WIN) + chunks(WIN, WIN + length):
                taps = taps_at(ys, mask_ref, at, tile)
                ws[at, tile] = (combine(w[1], taps) * combine(w[2], taps)).astype(BF)
                if at.start >= WIN:
                    qs[at.start - WIN : at.stop - WIN, tile] = combine(w[0], taps)
        z = dot(bt_ref[i], ws[:WIN, :]) + dot(b_ref[i], ws[WIN:, :])
        o_scr[i] = (qs[...] * z).astype(BF)
        copies.append(pltpu.make_async_copy(o_scr.at[i], out_ref.at[:, cols], sems.at[i]))
        copies[-1].start()
    for copy in copies:
        copy.wait()


def per_device(inputs, bounds, feat_first, li_decay, li_residue, feat_second, mr_filter):
    length, channels = inputs.shape
    groups, modes = li_decay.shape
    lanes = channels // groups
    filter_len = mr_filter.shape[1]
    rows = filter_len + 3
    cut = length - rows + 2
    size = lax.axis_size("seq")
    place = lax.axis_index("seq")

    def behind(array, by):
        return lax.ppermute(array, "seq", [(i, i + by) for i in range(size - by)])

    own_row = jnp.broadcast_to(bounds.astype(BF)[:, None], (1, channels))
    edge = behind(jnp.concatenate([inputs[length - 2 :], own_row], 0), 1)
    prior = jnp.where(place == 0, length, edge[2, 0].astype(F32).astype(jnp.int32))
    scal = jnp.stack([bounds[0], prior, (place % 2).astype(jnp.int32)])

    sm = pl.BlockSpec(memory_space=SMEM)
    whole = pl.BlockSpec(memory_space=pltpu.VMEM)
    params = pltpu.CompilerParams(vmem_limit_bytes=24 * 1024 * 1024)
    count = 2 if groups % 2 == 0 else 1
    steps, wide = groups // count, lanes * count

    def block(*shape):
        return pl.BlockSpec(shape, lambda g: (0,) * (len(shape) - 1) + (g,))

    def table(*shape):
        return pl.BlockSpec((count,) + shape, lambda g: (g, 0, 0))

    def single(*shape):
        return pl.BlockSpec((None,) + shape, lambda g: (g, 0, 0))

    def fixed(*shape):
        return pl.BlockSpec(shape, lambda g: (0,) * len(shape))

    mine, part, q_own, u_own = pl.pallas_call(
        functools.partial(states_kernel, cut, modes, lanes),
        in_specs=[sm] + [whole] * 4,
        out_specs=[whole] * 4,
        out_shape=[
            jax.ShapeDtypeStruct((modes, channels + LANE), BF),
            jax.ShapeDtypeStruct((modes, channels), BF),
            jax.ShapeDtypeStruct((length, channels), F32),
            jax.ShapeDtypeStruct((length, channels), BF),
        ],
        scratch_shapes=[
            pltpu.VMEM((2, length, LANE), F32), pltpu.VMEM((count, 8 + length, lanes), F32),
        ],
        compiler_params=params,
        cost_estimate=pl.CostEstimate(flops=10**8, bytes_accessed=2**16, transcendentals=0),
        name="states",
    )(scal, inputs, edge, feat_first, li_decay)
    other = lax.ppermute(mine, "seq", [(i, i ^ 1) for i in range(size)])
    inputs_late, part, other = lax.optimization_barrier((inputs, part, other))
    message = jnp.concatenate([part, inputs_late[length - rows :]], 0)
    message, other = lax.optimization_barrier((message, other))
    tail = behind(message, 1)
    pair = pl.pallas_call(
        functools.partial(pair_kernel, modes, length),
        in_specs=[sm] + [whole] * 3,
        out_specs=whole,
        out_shape=jax.ShapeDtypeStruct((2 * modes, channels + LANE), BF),
        compiler_params=params,
        name="pair",
    )(scal, mine, other, li_decay)
    near = lax.ppermute(pair, "seq", [(i, i + 2) for i in range(0, size - 2, 2)])
    far = [
        lax.ppermute(pair[:modes], "seq", [(i, i + by) for i in range(0, size - by, 2)])
        for by in range(4, size, 2)
    ]
    state_shape = jax.ShapeDtypeStruct((modes, channels), F32)
    send, even_own, even_late = pl.pallas_call(
        functools.partial(carry_kernel, modes, length),
        in_specs=[whole] * (2 + len(far)),
        out_specs=[whole] * 3,
        out_shape=[jax.ShapeDtypeStruct((modes, channels), BF), state_shape, state_shape],
        compiler_params=params,
        name="carry",
    )(near, li_decay, *far)
    sent = lax.ppermute(send, "seq", [(i, i + 1) for i in range(0, size, 2)])
    own_state, win_state = pl.pallas_call(
        functools.partial(place_kernel, cut, modes, length),
        in_specs=[sm] + [whole] * 6,
        out_specs=[whole] * 2,
        out_shape=[jax.ShapeDtypeStruct((3 * modes, channels), BF)] * 2,
        compiler_params=params,
        name="place",
    )(scal, other, tail, sent, even_own, even_late, li_decay)

    shapes = [
        (2 * length, length), (2 * WIN, WIN), (length, 3 * modes), (WIN, 3 * modes),
        (length, WIN), (length, length),
    ]
    t_own, t_win, r_own, r_win, b_win, b_own = pl.pallas_call(
        functools.partial(tables_kernel, cut, modes, length),
        grid=(groups,),
        in_specs=[sm, fixed(groups, modes), fixed(groups, modes), single(1, filter_len)],
        out_specs=[single(*s) for s in shapes],
        out_shape=[jax.ShapeDtypeStruct((groups,) + s, BF) for s in shapes],
        compiler_params=params,
        cost_estimate=pl.CostEstimate(flops=10**8, bytes_accessed=2**16, transcendentals=0),
        name="tables",
    )(scal, li_decay, li_residue, mr_filter.reshape(groups, 1, filter_len))

    q_win, u_win = pl.pallas_call(
        functools.partial(tail_kernel, modes, length, lanes),
        in_specs=[sm, whole, whole],
        out_specs=[whole] * 2,
        out_shape=[
            jax.ShapeDtypeStruct((WIN, channels), F32),
            jax.ShapeDtypeStruct((WIN, channels), BF),
        ],
        scratch_shapes=[
            pltpu.VMEM((2, WIN, LANE), F32), pltpu.VMEM((groups, 8 + WIN, lanes), F32),
        ],
        compiler_params=params,
        cost_estimate=pl.CostEstimate(flops=10**8, bytes_accessed=2**16, transcendentals=0),
        name="tail",
    )(scal, tail, feat_first)
    full = WIN + length
    return pl.pallas_call(
        functools.partial(final_kernel, lanes),
        in_specs=[sm] + [whole] * 13,
        out_specs=pl.BlockSpec(memory_space=pl.ANY),
        out_shape=jax.ShapeDtypeStruct((length, channels), BF),
        scratch_shapes=[
            pltpu.VMEM((2, full, LANE), F32), pltpu.VMEM((count, 8 + full, lanes), F32),
            pltpu.VMEM((count, full, lanes), BF), pltpu.VMEM((count, length, lanes), F32),
            pltpu.VMEM((count, full, lanes), F32), pltpu.VMEM((groups, length, lanes), BF),
            pltpu.SemaphoreType.DMA((groups,)),
        ],
        compiler_params=params,
        cost_estimate=pl.CostEstimate(flops=10**8, bytes_accessed=2**16, transcendentals=0),
        name="final",
    )(
        scal, q_own, u_own, q_win, u_win, t_own, t_win, r_own, r_win, own_state, win_state,
        feat_second, b_win, b_own,
    )


def solution(mesh):
    in_specs = (
        P(("groups", "seq"), "chan"),
        P(("groups", "seq")),
        P(None, None, "chan"),
        P("chan", None),
        P("chan", None),
        P(None, None, "chan"),
        P("chan", None),
    )
    out_specs = P(("groups", "seq"), "chan")
    return jax.shard_map(
        per_device, mesh=mesh, in_specs=in_specs, out_specs=out_specs, check_vma=False
    )
```

```python
import functools
import math

import jax
import jax.numpy as jnp
from jax import lax
from jax.experimental import pallas as pl
from jax.experimental.pallas import tpu as pltpu
from jax.sharding import PartitionSpec as P

F32 = jnp.float32
BF = jnp.bfloat16
WIN = 144
LANE = 128
CHUNK = 32
SMEM = pltpu.SMEM


def dot(a, b):
    return lax.dot_general(a, b, (((1,), (0,)), ((), ())), preferred_element_type=F32)


def iota(shape, dim):
    return lax.broadcasted_iota(jnp.int32, shape, dim)


def column(row):
    n = row.shape[1]
    return jnp.sum(
        jnp.where(iota((n, n), 0) == iota((n, n), 1), row, 0.0), axis=1, keepdims=True
    )


def one(cond):
    return jnp.where(cond, 1.0, 0.0).astype(BF)


def weights_of(w_ref, cols):
    return [[w_ref[b, o : o + 1, cols] for o in range(3)] for b in range(3)]


def combine(w, taps):
    return w[0] * taps[0] + w[1] * taps[1] + w[2] * taps[2]


def taps_at(ref, mask_ref, at, cols):
    rows = ref[at.start : at.stop + 8, cols]
    return (
        rows[8:],
        pltpu.roll(rows, 1, 0)[8:] * mask_ref[0, at, :],
        pltpu.roll(rows, 2, 0)[8:] * mask_ref[1, at, :],
    )


def taps_of(prev, rows, mask_ref, at):
    both = jnp.concatenate([prev, rows], 0)
    return (
        rows,
        pltpu.roll(both, 1, 0)[8:] * mask_ref[0, at, :],
        pltpu.roll(both, 2, 0)[8:] * mask_ref[1, at, :],
    )


def chunks(first, last, rows=CHUNK):
    return [slice(r, min(r + rows, last)) for r in range(first, last, rows)]


def tiles(lanes):
    return [slice(c, c + LANE) for c in range(0, lanes, LANE)]


def spans(count, lanes):
    return [(i, slice(i * lanes, (i + 1) * lanes)) for i in range(count)]


def write_masks(ref, offset, own, prior, length):
    rows = ref.shape[1]
    t = iota((rows, LANE), 0) - offset
    before = jnp.where(prior < length, prior, -length) - length
    one_back = (t != own) & (t != before)
    two_back = one_back & (t - 1 != own) & (t - 1 != before)
    ref[0] = jnp.where(one_back, 1.0, 0.0)
    ref[1] = jnp.where(two_back, 1.0, 0.0)


def split(v):
    hi = v.astype(BF)
    return hi, (v - hi.astype(F32)).astype(BF)


def load_kernel(bounds, x_ref, w_ref, dec_ref, x_out, w_out, dec_out, edge_out, sems):
    pairs = ((x_ref, x_out), (w_ref, w_out), (dec_ref, dec_out))
    copies = [pltpu.make_async_copy(a, b, sems.at[i]) for i, (a, b) in enumerate(pairs)]
    for copy in copies:
        copy.start()
    for copy in copies:
        copy.wait()
    length, width = x_out.shape
    last = x_out[length - 16 :, :].astype(F32)[14:]
    own = jnp.full((1, width), bounds[0], jnp.int32).astype(F32)
    edge_out[...] = jnp.concatenate([last, own], 0).astype(BF)


def states_kernel(
    cut, modes, lanes, bounds, x_ref, edge_ref, w_ref, dec_ref, out_ref, part_ref, q_ref, u_ref,
    scal_ref, mask_ref,
):
    length, width = x_ref.shape
    own = bounds[0]
    place = lax.axis_index("seq")
    told = jnp.max(edge_ref[...].astype(F32)[2:3, :LANE]).astype(jnp.int32)
    prior = jnp.where(place == 0, length, told)
    scal_ref[0] = own
    scal_ref[1] = prior
    scal_ref[2] = place % 2
    write_masks(mask_ref, 0, own, prior, length)
    flag = jnp.full((modes, LANE), own, jnp.int32).astype(F32)
    out_ref[:, width:] = flag.astype(BF)

    p = iota((modes, length), 1)
    lag = (length - 1 - p).astype(F32)
    lag_cut = jnp.maximum(cut - 1 - p, 0).astype(F32)
    reach = (p >= own) | (own >= length)
    reach_cut = (p < cut) & ((p >= own) | (own >= cut))
    for i, cols in spans(width // lanes, lanes):
        for tile in tiles(lanes):
            here = slice(cols.start + tile.start, cols.start + tile.stop)
            w = weights_of(w_ref, here)
            edge = edge_ref[:, here].astype(F32)
            prev = jnp.concatenate([jnp.zeros((6, LANE), F32), edge[:2]], 0)
            for at in chunks(0, length):
                x = x_ref[at, here].astype(F32)
                taps = taps_of(prev, x, mask_ref, at)
                prev = x[-8:]
                u_ref[at, here] = (combine(w[1], taps) * combine(w[2], taps)).astype(BF)
                q_ref[at, here] = combine(w[0], taps)
        dec = column(dec_ref[i : i + 1, :])
        full = jnp.where(reach, jnp.exp(-dec * lag), 0.0)
        part = jnp.where(reach_cut, jnp.exp(-dec * lag_cut), 0.0)
        hi, lo = split(jnp.concatenate([full, part], 0))
        both = dot(jnp.concatenate([hi, lo], 0), u_ref[:, cols])
        state = both[: 2 * modes] + both[2 * modes :]
        out_ref[:, cols] = state[:modes].astype(BF)
        part_ref[:, cols] = state[modes:].astype(BF)


def pair_kernel(modes, length, scal, mine_ref, other_ref, dec_ref, out_ref):
    groups = dec_ref.shape[0]
    width = mine_ref.shape[1] - LANE
    lanes = width // groups
    even = scal[2] == 0
    end = slice(width, width + LANE)

    def pick(cols):
        a, b = mine_ref[:, cols].astype(F32), other_ref[:, cols].astype(F32)
        return jnp.where(even, a, b), jnp.where(even, b, a)

    top, low = slice(0, modes), slice(modes, 2 * modes)
    f_bound, s_bound = pick(end)
    free_f = jnp.where(f_bound >= length, 1.0, 0.0)
    free_s = jnp.where(s_bound >= length, 1.0, 0.0)
    out_ref[top, end] = (free_f * free_s).astype(BF)
    out_ref[low, end] = free_f.astype(BF)
    for g in range(groups):
        cols = slice(g * lanes, (g + 1) * lanes)
        dec = column(dec_ref[g : g + 1, :])
        first, second = pick(cols)
        out_ref[top, cols] = (second + jnp.exp(-dec * length) * free_s[:, :1] * first).astype(BF)
        out_ref[low, cols] = first.astype(BF)


def carry_kernel(modes, length, near_ref, dec_ref, *refs):
    far, (send_ref, own_ref, late_ref) = refs[:-3], refs[-3:]
    groups = dec_ref.shape[0]
    width = own_ref.shape[1]
    lanes = width // groups
    top, low = slice(0, modes), slice(modes, 2 * modes)
    near_free = near_ref[top, width : width + LANE].astype(F32)[:, :1]
    late_free = near_ref[low, width : width + LANE].astype(F32)[:, :1]
    far_free = [f[:, width : width + LANE].astype(F32)[:, :1] for f in far]
    for g in range(groups):
        cols = slice(g * lanes, (g + 1) * lanes)
        dec = column(dec_ref[g : g + 1, :])
        once = jnp.exp(-dec * length)
        pair = jnp.exp(-dec * (2 * length))
        behind = jnp.zeros((modes, lanes), F32)
        for f, free in zip(far[::-1], far_free[::-1]):
            behind = f[:, cols].astype(F32) + pair * free * behind
        whole = near_ref[top, cols].astype(F32) + pair * near_free * behind
        send_ref[:, cols] = whole.astype(BF)
        own_ref[:, cols] = whole
        late_ref[:, cols] = near_ref[low, cols].astype(F32) + once * late_free * behind


def place_kernel(
    cut, modes, length, scal, other_ref, part_ref, sent_ref, even_own, even_late, dec_ref,
    own_ref, win_ref,
):
    groups = dec_ref.shape[0]
    lanes = own_ref.shape[1] // groups
    even = scal[2] == 0
    prior = scal[1]
    pass_own = jnp.where(prior >= length, 1.0, 0.0)
    pass_cut = jnp.where(prior >= cut, 1.0, 0.0)
    for g in range(groups):
        cols = slice(g * lanes, (g + 1) * lanes)
        dec = column(dec_ref[g : g + 1, :])
        sent = sent_ref[:, cols].astype(F32)
        odd_own = other_ref[:, cols].astype(F32) + jnp.exp(-dec * length) * pass_own * sent
        before = jnp.where(even, even_late[:, cols], sent)
        own = jnp.where(even, even_own[:, cols], odd_own)
        win = part_ref[: dec_ref.shape[1], cols].astype(F32) + jnp.exp(-dec * cut) * pass_cut * before
        for ref, v in ((own_ref, own), (win_ref, win)):
            hi, lo = split(v)
            ref[:, cols] = jnp.concatenate([hi, lo, hi], 0)


def tables_kernel(cut, modes, length, scal, dec_ref, res_ref, mr_ref, *outs):
    t_own, t_win, r_own, r_win, b_win, b_own = outs
    g = pl.program_id(0)
    own, prior = scal[0], scal[1]
    wide = 2 * length
    base = length - WIN
    dec_row = dec_ref[pl.ds(g, 1), :]
    weight_row = res_ref[pl.ds(g, 1), :] * jnp.sqrt(
        jnp.maximum(1.0 - jnp.exp(-2.0 * dec_row), 0.0)
    ) / math.sqrt(modes)
    small = 2.0 * dec_row
    series = small * (1.0 - small * (0.5 - small * (1.0 / 6 - small * (1.0 / 24))))
    weight_row = jnp.where(
        small < 0.05,
        res_ref[pl.ds(g, 1), :] * jnp.sqrt(series) / math.sqrt(modes),
        weight_row,
    )
    dec, weight = column(dec_row), column(weight_row)
    back = iota((modes, wide), 1)
    back = jnp.where(back == 0, 0, wide - back).astype(F32)
    taps = jnp.sum(weight * jnp.exp(-dec * back), axis=0, keepdims=True)
    full = pltpu.roll(jnp.broadcast_to(taps, (length, wide)), 0, 1, stride=1, stride_axis=0)
    t, p = iota((length, length), 0), iota((length, length), 1)
    seen = (p <= t) & ((p >= own) == (t >= own))
    t_own[:length, :], t_own[length:, :] = split(jnp.where(seen, full[:, :length], 0.0))
    tw, pw = iota((WIN, WIN), 0) + base, iota((WIN, WIN), 1) + base
    seen = (pw <= tw) & (pw >= cut) & ((pw >= prior) == (tw >= prior))
    t_win[:WIN, :], t_win[WIN:, :] = split(jnp.where(seen, full[:WIN, :WIN], 0.0))

    tl = iota((modes, length), 1)
    rise = jnp.where(tl < own, weight * jnp.exp(-dec * (tl + 1).astype(F32)), 0.0)
    wl = tl + base
    lag = jnp.maximum(wl - cut + 1, 0)
    fits = (wl >= cut) & ((prior < cut) | (prior > wl))
    rise_w = jnp.where(fits, weight * jnp.exp(-dec * lag.astype(F32)), 0.0)
    for ref, v, rows in ((r_own, rise, length), (r_win, rise_w, WIN)):
        hi = v.astype(BF).astype(F32)
        stack = jnp.concatenate([hi, hi, v - hi, jnp.zeros((LANE - 3 * modes, length), F32)], 0)
        ref[...] = jnp.transpose(stack)[:rows, : 3 * modes].astype(BF)

    count = mr_ref.shape[1]
    o, n = iota((count, wide), 0), iota((count, wide), 1)
    back = dot(mr_ref[...], one(((n == 0) & (o == 0)) | ((n > 0) & (wide - n == o))))
    band = pltpu.roll(
        jnp.broadcast_to(back, (WIN + length, wide)), 0, 1, stride=1, stride_axis=0
    )
    seen = (p <= t) & ((p >= own) == (t >= own))
    b_own[...] = jnp.where(seen, band[:length, :length], 0.0).astype(BF)
    tb, pb = iota((length, WIN), 0), iota((length, WIN), 1) + base
    seen = (tb < own) & ((prior >= length) | (pb >= prior))
    b_win[...] = jnp.where(seen, band[WIN : WIN + length, :WIN], 0.0).astype(BF)


def tail_kernel(
    modes, length, lanes, scal, tail_ref, w_ref, t_ref, q_ref, z_ref, mask_ref, x_scr, u_scr
):
    rows = tail_ref.shape[0] - modes

    write_masks(mask_ref, WIN, scal[0], scal[1], length)
    x_scr[:, : 8 + WIN - rows, :] = jnp.zeros(
        (x_scr.shape[0], 8 + WIN - rows, x_scr.shape[2]), F32
    )

    for i, cols in spans(tail_ref.shape[1] // lanes, lanes):
        scr, us = x_scr.at[i], u_scr.at[i]
        scr[8 + WIN - rows : 8 + WIN, :] = tail_ref[modes:, cols].astype(F32)
        for tile in tiles(lanes):
            here = slice(cols.start + tile.start, cols.start + tile.stop)
            w = weights_of(w_ref, here)
            for at in chunks(0, WIN):
                taps = taps_at(scr, mask_ref, at, tile)
                us[at, tile] = (combine(w[1], taps) * combine(w[2], taps)).astype(BF)
                q_ref[at, here] = combine(w[0], taps)
        near = dot(t_ref[i], us[...])
        z_ref[:, cols] = near[:WIN] + near[WIN:]


def near_kernel(lanes, u_ref, t_ref, z_ref):
    length = u_ref.shape[0]
    for i, cols in spans(u_ref.shape[1] // lanes, lanes):
        near = dot(t_ref[i], u_ref[:, cols])
        z_ref[:, cols] = near[:length] + near[length:]


def final_kernel(
    lanes, scal, q_ref, z_ref, qt_ref, zt_ref, r_ref, rt_ref, st_ref, stt_ref,
    w_ref, bt_ref, b_ref, out_ref, mask_ref, w_scr, q_scr, z_scr, o_scr, sems,
):
    length = q_ref.shape[0]

    write_masks(mask_ref, WIN, scal[0], scal[1], length)
    copies = []
    for i, cols in spans(q_ref.shape[1] // lanes, lanes):
        k = i % w_scr.shape[0]
        ws, qs, zs = w_scr.at[k], q_scr.at[k], z_scr.at[k]
        zs[:WIN, :] = dot(rt_ref[i], stt_ref[:, cols])
        zs[WIN:, :] = dot(r_ref[i], st_ref[:, cols])
        for tile in tiles(lanes):
            here = slice(cols.start + tile.start, cols.start + tile.stop)
            w = weights_of(w_ref, here)
            prev = jnp.zeros((8, LANE), F32)
            for at in chunks(0, WIN) + chunks(WIN, WIN + length):
                if at.start < WIN:
                    q, z = qt_ref[at, here], zt_ref[at, here]
                else:
                    part = slice(at.start - WIN, at.stop - WIN)
                    q, z = q_ref[part, here], z_ref[part, here]
                y = (q * (z + zs[at, tile])).astype(BF).astype(F32)
                taps = taps_of(prev, y, mask_ref, at)
                prev = y[-8:]
                ws[at, tile] = (combine(w[1], taps) * combine(w[2], taps)).astype(BF)
                if at.start >= WIN:
                    qs[at.start - WIN : at.stop - WIN, tile] = combine(w[0], taps)
        z = dot(bt_ref[i], ws[:WIN, :]) + dot(b_ref[i], ws[WIN:, :])
        o_scr[i] = (qs[...] * z).astype(BF)
        copies.append(pltpu.make_async_copy(o_scr.at[i], out_ref.at[:, cols], sems.at[i]))
        copies[-1].start()
    for copy in copies:
        copy.wait()


def per_device(inputs, bounds, feat_first, li_decay, li_residue, feat_second, mr_filter):
    length, channels = inputs.shape
    groups, modes = li_decay.shape
    lanes = channels // groups
    filter_len = mr_filter.shape[1]
    rows = filter_len + 3
    cut = length - rows + 2
    size = lax.axis_size("seq")

    def behind(array, by):
        return lax.ppermute(array, "seq", [(i, i + by) for i in range(size - by)])

    sm = pl.BlockSpec(memory_space=SMEM)
    whole = pl.BlockSpec(memory_space=pltpu.VMEM)
    params = pltpu.CompilerParams(vmem_limit_bytes=24 * 1024 * 1024)
    count = 2 if groups % 2 == 0 else 1
    steps, wide = groups // count, lanes * count

    hbm = pl.BlockSpec(memory_space=pl.ANY)
    held, held_first, held_decay, edge = pl.pallas_call(
        load_kernel,
        in_specs=[sm] + [hbm] * 3,
        out_specs=[whole] * 4,
        out_shape=[jax.ShapeDtypeStruct(a.shape, a.dtype) for a in (inputs, feat_first, li_decay)]
        + [jax.ShapeDtypeStruct((3, channels), BF)],
        scratch_shapes=[pltpu.SemaphoreType.DMA((3,))],
        compiler_params=pltpu.CompilerParams(vmem_limit_bytes=50 * 1024 * 1024),
        name="load",
    )(bounds, inputs, feat_first, li_decay)
    edge = behind(edge, 1)
    def block(*shape):
        return pl.BlockSpec(shape, lambda g: (0,) * (len(shape) - 1) + (g,))

    def table(*shape):
        return pl.BlockSpec((count,) + shape, lambda g: (g, 0, 0))

    def single(*shape):
        return pl.BlockSpec((None,) + shape, lambda g: (g, 0, 0))

    def fixed(*shape):
        return pl.BlockSpec(shape, lambda g: (0,) * len(shape))

    mine, part, q_own, u_own, scal = pl.pallas_call(
        functools.partial(states_kernel, cut, modes, lanes),
        in_specs=[sm] + [whole] * 4,
        out_specs=[whole] * 4 + [sm],
        out_shape=[
            jax.ShapeDtypeStruct((modes, channels + LANE), BF),
            jax.ShapeDtypeStruct((modes, channels), BF),
            jax.ShapeDtypeStruct((length, channels), F32),
            jax.ShapeDtypeStruct((length, channels), BF),
            jax.ShapeDtypeStruct((3,), jnp.int32),
        ],
        scratch_shapes=[
            pltpu.VMEM((2, length, LANE), F32),
        ],
        compiler_params=params,
        cost_estimate=pl.CostEstimate(flops=10**8, bytes_accessed=2**16, transcendentals=0),
        name="states",
    )(bounds, held, edge, held_first, held_decay)
    other = lax.ppermute(mine, "seq", [(i, i ^ 1) for i in range(size)])
    inputs_late, part, other = lax.optimization_barrier((held, part, other))
    message = jnp.concatenate([part, inputs_late[length - rows :]], 0)
    message, other = lax.optimization_barrier((message, other))
    tail = behind(message, 1)
    pair = pl.pallas_call(
        functools.partial(pair_kernel, modes, length),
        in_specs=[sm] + [whole] * 3,
        out_specs=whole,
        out_shape=jax.ShapeDtypeStruct((2 * modes, channels + LANE), BF),
        compiler_params=params,
        name="pair",
    )(scal, mine, other, held_decay)
    near = lax.ppermute(pair, "seq", [(i, i + 2) for i in range(0, size - 2, 2)])
    far = [
        lax.ppermute(pair[:modes], "seq", [(i, i + by) for i in range(0, size - by, 2)])
        for by in range(4, size, 2)
    ]
    state_shape = jax.ShapeDtypeStruct((modes, channels), F32)
    send, even_own, even_late = pl.pallas_call(
        functools.partial(carry_kernel, modes, length),
        in_specs=[whole] * (2 + len(far)),
        out_specs=[whole] * 3,
        out_shape=[jax.ShapeDtypeStruct((modes, channels), BF), state_shape, state_shape],
        compiler_params=params,
        name="carry",
    )(near, held_decay, *far)
    sent = lax.ppermute(send, "seq", [(i, i + 1) for i in range(0, size, 2)])
    own_state, win_state = pl.pallas_call(
        functools.partial(place_kernel, cut, modes, length),
        in_specs=[sm] + [whole] * 6,
        out_specs=[whole] * 2,
        out_shape=[jax.ShapeDtypeStruct((3 * modes, channels), BF)] * 2,
        compiler_params=params,
        name="place",
    )(scal, other, tail, sent, even_own, even_late, held_decay)

    shapes = [
        (2 * length, length), (2 * WIN, WIN), (length, 3 * modes), (WIN, 3 * modes),
        (length, WIN), (length, length),
    ]
    t_own, t_win, r_own, r_win, b_win, b_own = pl.pallas_call(
        functools.partial(tables_kernel, cut, modes, length),
        grid=(groups,),
        in_specs=[sm, fixed(groups, modes), fixed(groups, modes), single(1, filter_len)],
        out_specs=[single(*s) for s in shapes],
        out_shape=[jax.ShapeDtypeStruct((groups,) + s, BF) for s in shapes],
        compiler_params=params,
        cost_estimate=pl.CostEstimate(flops=10**8, bytes_accessed=2**16, transcendentals=0),
        name="tables",
    )(scal, li_decay, li_residue, mr_filter.reshape(groups, 1, filter_len))

    z_own = pl.pallas_call(
        functools.partial(near_kernel, lanes),
        in_specs=[whole] * 2,
        out_specs=whole,
        out_shape=jax.ShapeDtypeStruct((length, channels), F32),
        compiler_params=params,
        cost_estimate=pl.CostEstimate(flops=10**8, bytes_accessed=2**16, transcendentals=0),
        name="near",
    )(u_own, t_own)
    q_win, z_win = pl.pallas_call(
        functools.partial(tail_kernel, modes, length, lanes),
        in_specs=[sm] + [whole] * 3,
        out_specs=[whole] * 2,
        out_shape=[
            jax.ShapeDtypeStruct((WIN, channels), F32),
            jax.ShapeDtypeStruct((WIN, channels), F32),
        ],
        scratch_shapes=[
            pltpu.VMEM((2, WIN, LANE), F32), pltpu.VMEM((groups, 8 + WIN, lanes), F32),
            pltpu.VMEM((groups, WIN, lanes), BF),
        ],
        compiler_params=params,
        cost_estimate=pl.CostEstimate(flops=10**8, bytes_accessed=2**16, transcendentals=0),
        name="tail",
    )(scal, tail, held_first, t_win)
    full = WIN + length
    return pl.pallas_call(
        functools.partial(final_kernel, lanes),
        in_specs=[sm] + [whole] * 11,
        out_specs=pl.BlockSpec(memory_space=pl.ANY),
        out_shape=jax.ShapeDtypeStruct((length, channels), BF),
        scratch_shapes=[
            pltpu.VMEM((2, full, LANE), F32),
            pltpu.VMEM((count, full, lanes), BF), pltpu.VMEM((count, length, lanes), F32),
            pltpu.VMEM((count, full, lanes), F32), pltpu.VMEM((groups, length, lanes), BF),
            pltpu.SemaphoreType.DMA((groups,)),
        ],
        compiler_params=params,
        cost_estimate=pl.CostEstimate(flops=10**8, bytes_accessed=2**16, transcendentals=0),
        name="final",
    )(
        scal, q_own, z_own, q_win, z_win, r_own, r_win, own_state, win_state,
        feat_second, b_win, b_own,
    )


def solution(mesh):
    in_specs = (
        P(("groups", "seq"), "chan"),
        P(("groups", "seq")),
        P(None, None, "chan"),
        P("chan", None),
        P("chan", None),
        P(None, None, "chan"),
        P("chan", None),
    )
    out_specs = P(("groups", "seq"), "chan")
    return jax.shard_map(
        per_device, mesh=mesh, in_specs=in_specs, out_specs=out_specs, check_vma=False
    )
```

```python
import functools
import math

import jax
import jax.numpy as jnp
from jax import lax
from jax.experimental import pallas as pl
from jax.experimental.pallas import tpu as pltpu
from jax.sharding import PartitionSpec as P

F32 = jnp.float32
BF = jnp.bfloat16
WIN = 144
LANE = 128
CHUNK = 32
SMEM = pltpu.SMEM


def dot(a, b):
    return lax.dot_general(a, b, (((1,), (0,)), ((), ())), preferred_element_type=F32)


def iota(shape, dim):
    return lax.broadcasted_iota(jnp.int32, shape, dim)


def column(row):
    n = row.shape[1]
    return jnp.sum(
        jnp.where(iota((n, n), 0) == iota((n, n), 1), row, 0.0), axis=1, keepdims=True
    )


def one(cond):
    return jnp.where(cond, 1.0, 0.0).astype(BF)


def weights_of(w_ref, cols):
    return [[w_ref[b, o : o + 1, cols] for o in range(3)] for b in range(3)]


def combine(w, taps):
    return w[0] * taps[0] + w[1] * taps[1] + w[2] * taps[2]


def taps_at(ref, mask_ref, at, cols):
    rows = ref[at.start : at.stop + 8, cols]
    return (
        rows[8:],
        pltpu.roll(rows, 1, 0)[8:] * mask_ref[0, at, :],
        pltpu.roll(rows, 2, 0)[8:] * mask_ref[1, at, :],
    )


def taps_of(prev, rows, mask_ref, at):
    both = jnp.concatenate([prev, rows], 0)
    return (
        rows,
        pltpu.roll(both, 1, 0)[8:] * mask_ref[0, at, :],
        pltpu.roll(both, 2, 0)[8:] * mask_ref[1, at, :],
    )


def chunks(first, last, rows=CHUNK):
    return [slice(r, min(r + rows, last)) for r in range(first, last, rows)]


def tiles(lanes):
    return [slice(c, c + LANE) for c in range(0, lanes, LANE)]


def spans(count, lanes):
    return [(i, slice(i * lanes, (i + 1) * lanes)) for i in range(count)]


def write_masks(ref, offset, own, prior, length):
    rows = ref.shape[1]
    t = iota((rows, LANE), 0) - offset
    before = jnp.where(prior < length, prior, -length) - length
    one_back = (t != own) & (t != before)
    two_back = one_back & (t - 1 != own) & (t - 1 != before)
    ref[0] = jnp.where(one_back, 1.0, 0.0)
    ref[1] = jnp.where(two_back, 1.0, 0.0)


def split(v):
    hi = v.astype(BF)
    return hi, (v - hi.astype(F32)).astype(BF)


def load_kernel(bounds, x_ref, w_ref, dec_ref, x_out, w_out, dec_out, edge_out, sems):
    pairs = ((x_ref, x_out), (w_ref, w_out), (dec_ref, dec_out))
    copies = [pltpu.make_async_copy(a, b, sems.at[i]) for i, (a, b) in enumerate(pairs)]
    for copy in copies:
        copy.start()
    for copy in copies:
        copy.wait()
    length, width = x_out.shape
    last = x_out[length - 16 :, :].astype(F32)[14:]
    own = jnp.full((1, width), bounds[0], jnp.int32).astype(F32)
    edge_out[...] = jnp.concatenate([last, own], 0).astype(BF)


def states_kernel(
    cut, modes, lanes, bounds, x_ref, edge_ref, w_ref, dec_ref, out_ref, part_ref, q_ref, u_ref,
    scal_ref, mask_ref,
):
    length, width = x_ref.shape
    own = bounds[0]
    place = lax.axis_index("seq")
    told = jnp.max(edge_ref[...].astype(F32)[2:3, :LANE]).astype(jnp.int32)
    prior = jnp.where(place == 0, length, told)
    scal_ref[0] = own
    scal_ref[1] = prior
    scal_ref[2] = place % 2
    write_masks(mask_ref, 0, own, prior, length)
    flag = jnp.full((modes, LANE), own, jnp.int32).astype(F32)
    out_ref[:, width:] = flag.astype(BF)

    p = iota((modes, length), 1)
    lag = (length - 1 - p).astype(F32)
    lag_cut = jnp.maximum(cut - 1 - p, 0).astype(F32)
    reach = (p >= own) | (own >= length)
    reach_cut = (p < cut) & ((p >= own) | (own >= cut))
    for i, cols in spans(width // lanes, lanes):
        for tile in tiles(lanes):
            here = slice(cols.start + tile.start, cols.start + tile.stop)
            w = weights_of(w_ref, here)
            edge = edge_ref[:, here].astype(F32)
            prev = jnp.concatenate([jnp.zeros((6, LANE), F32), edge[:2]], 0)
            for at in chunks(0, length):
                x = x_ref[at, here].astype(F32)
                taps = taps_of(prev, x, mask_ref, at)
                prev = x[-8:]
                u_ref[at, here] = (combine(w[1], taps) * combine(w[2], taps)).astype(BF)
                q_ref[at, here] = combine(w[0], taps)
        dec = column(dec_ref[i : i + 1, :])
        full = jnp.where(reach, jnp.exp(-dec * lag), 0.0)
        part = jnp.where(reach_cut, jnp.exp(-dec * lag_cut), 0.0)
        hi, lo = split(jnp.concatenate([full, part], 0))
        both = dot(jnp.concatenate([hi, lo], 0), u_ref[:, cols])
        state = both[: 2 * modes] + both[2 * modes :]
        out_ref[:, cols] = state[:modes].astype(BF)
        part_ref[:, cols] = state[modes:].astype(BF)


def pair_kernel(modes, length, scal, mine_ref, other_ref, dec_ref, out_ref):
    groups = dec_ref.shape[0]
    width = mine_ref.shape[1] - LANE
    lanes = width // groups
    even = scal[2] == 0
    end = slice(width, width + LANE)

    def pick(cols):
        a, b = mine_ref[:, cols].astype(F32), other_ref[:, cols].astype(F32)
        return jnp.where(even, a, b), jnp.where(even, b, a)

    top, low = slice(0, modes), slice(modes, 2 * modes)
    f_bound, s_bound = pick(end)
    free_f = jnp.where(f_bound >= length, 1.0, 0.0)
    free_s = jnp.where(s_bound >= length, 1.0, 0.0)
    out_ref[top, end] = (free_f * free_s).astype(BF)
    out_ref[low, end] = free_f.astype(BF)
    for g in range(groups):
        cols = slice(g * lanes, (g + 1) * lanes)
        dec = column(dec_ref[g : g + 1, :])
        first, second = pick(cols)
        out_ref[top, cols] = (second + jnp.exp(-dec * length) * free_s[:, :1] * first).astype(BF)
        out_ref[low, cols] = first.astype(BF)


def carry_kernel(modes, length, near_ref, dec_ref, *refs):
    far, (send_ref, own_ref, late_ref) = refs[:-3], refs[-3:]
    groups = dec_ref.shape[0]
    width = own_ref.shape[1]
    lanes = width // groups
    top, low = slice(0, modes), slice(modes, 2 * modes)
    near_free = near_ref[top, width : width + LANE].astype(F32)[:, :1]
    late_free = near_ref[low, width : width + LANE].astype(F32)[:, :1]
    far_free = [f[:, width : width + LANE].astype(F32)[:, :1] for f in far]
    for g in range(groups):
        cols = slice(g * lanes, (g + 1) * lanes)
        dec = column(dec_ref[g : g + 1, :])
        once = jnp.exp(-dec * length)
        pair = jnp.exp(-dec * (2 * length))
        behind = jnp.zeros((modes, lanes), F32)
        for f, free in zip(far[::-1], far_free[::-1]):
            behind = f[:, cols].astype(F32) + pair * free * behind
        whole = near_ref[top, cols].astype(F32) + pair * near_free * behind
        send_ref[:, cols] = whole.astype(BF)
        own_ref[:, cols] = whole
        late_ref[:, cols] = near_ref[low, cols].astype(F32) + once * late_free * behind


def place_kernel(
    cut, modes, length, scal, other_ref, part_ref, sent_ref, even_own, even_late, dec_ref,
    own_ref, win_ref,
):
    groups = dec_ref.shape[0]
    lanes = own_ref.shape[1] // groups
    even = scal[2] == 0
    prior = scal[1]
    pass_own = jnp.where(prior >= length, 1.0, 0.0)
    pass_cut = jnp.where(prior >= cut, 1.0, 0.0)
    for g in range(groups):
        cols = slice(g * lanes, (g + 1) * lanes)
        dec = column(dec_ref[g : g + 1, :])
        sent = sent_ref[:, cols].astype(F32)
        odd_own = other_ref[:, cols].astype(F32) + jnp.exp(-dec * length) * pass_own * sent
        before = jnp.where(even, even_late[:, cols], sent)
        own = jnp.where(even, even_own[:, cols], odd_own)
        win = part_ref[: dec_ref.shape[1], cols].astype(F32) + jnp.exp(-dec * cut) * pass_cut * before
        for ref, v in ((own_ref, own), (win_ref, win)):
            hi, lo = split(v)
            ref[:, cols] = jnp.concatenate([hi, lo, hi], 0)


def tables_kernel(cut, modes, length, scal, dec_ref, res_ref, mr_ref, *outs):
    t_own, t_win, r_own, r_win, b_all = outs
    g = pl.program_id(0)
    own, prior = scal[0], scal[1]
    wide = 2 * length
    base = length - WIN
    dec_row = dec_ref[pl.ds(g, 1), :]
    weight_row = res_ref[pl.ds(g, 1), :] * jnp.sqrt(
        jnp.maximum(1.0 - jnp.exp(-2.0 * dec_row), 0.0)
    ) / math.sqrt(modes)
    small = 2.0 * dec_row
    series = small * (1.0 - small * (0.5 - small * (1.0 / 6 - small * (1.0 / 24))))
    weight_row = jnp.where(
        small < 0.05,
        res_ref[pl.ds(g, 1), :] * jnp.sqrt(series) / math.sqrt(modes),
        weight_row,
    )
    dec, weight = column(dec_row), column(weight_row)
    back = iota((modes, wide), 1)
    back = jnp.where(back == 0, 0, wide - back).astype(F32)
    taps = jnp.sum(weight * jnp.exp(-dec * back), axis=0, keepdims=True)
    full = pltpu.roll(jnp.broadcast_to(taps, (length, wide)), 0, 1, stride=1, stride_axis=0)
    t, p = iota((length, length), 0), iota((length, length), 1)
    seen = (p <= t) & ((p >= own) == (t >= own))
    t_own[:length, :], t_own[length:, :] = split(jnp.where(seen, full[:, :length], 0.0))
    tw, pw = iota((WIN, WIN), 0) + base, iota((WIN, WIN), 1) + base
    seen = (pw <= tw) & (pw >= cut) & ((pw >= prior) == (tw >= prior))
    t_win[:WIN, :], t_win[WIN:, :] = split(jnp.where(seen, full[:WIN, :WIN], 0.0))

    tl = iota((modes, length), 1)
    rise = jnp.where(tl < own, weight * jnp.exp(-dec * (tl + 1).astype(F32)), 0.0)
    wl = tl + base
    lag = jnp.maximum(wl - cut + 1, 0)
    fits = (wl >= cut) & ((prior < cut) | (prior > wl))
    rise_w = jnp.where(fits, weight * jnp.exp(-dec * lag.astype(F32)), 0.0)
    for ref, v, rows in ((r_own, rise, length), (r_win, rise_w, WIN)):
        hi = v.astype(BF).astype(F32)
        stack = jnp.concatenate([hi, hi, v - hi, jnp.zeros((LANE - 3 * modes, length), F32)], 0)
        ref[...] = jnp.transpose(stack)[:rows, : 3 * modes].astype(BF)

    count = mr_ref.shape[1]
    o, n = iota((count, wide), 0), iota((count, wide), 1)
    back = dot(mr_ref[...], one(((n == 0) & (o == 0)) | ((n > 0) & (wide - n == o))))
    band = pltpu.roll(
        jnp.broadcast_to(back, (2 * count, wide)), 0, 1, stride=1, stride_axis=0
    )[count:, : 2 * count]
    for first in range(0, length, count):
        t = iota((count, 2 * count), 0) + first
        p = iota((count, 2 * count), 1) + (first - count)
        same = (p >= own) == (t >= own)
        early = (p >= 0) | (prior >= length) | (p + length >= prior)
        b_all[first : first + count, :] = jnp.where(same & early, band, 0.0).astype(BF)


def tail_kernel(
    modes, length, lanes, scal, tail_ref, w_ref, t_ref, q_ref, z_ref, mask_ref, x_scr, u_scr
):
    rows = tail_ref.shape[0] - modes

    write_masks(mask_ref, WIN, scal[0], scal[1], length)
    x_scr[:, : 8 + WIN - rows, :] = jnp.zeros(
        (x_scr.shape[0], 8 + WIN - rows, x_scr.shape[2]), F32
    )

    for i, cols in spans(tail_ref.shape[1] // lanes, lanes):
        scr, us = x_scr.at[i], u_scr.at[i]
        scr[8 + WIN - rows : 8 + WIN, :] = tail_ref[modes:, cols].astype(F32)
        for tile in tiles(lanes):
            here = slice(cols.start + tile.start, cols.start + tile.stop)
            w = weights_of(w_ref, here)
            for at in chunks(0, WIN):
                taps = taps_at(scr, mask_ref, at, tile)
                us[at, tile] = (combine(w[1], taps) * combine(w[2], taps)).astype(BF)
                q_ref[at, here] = combine(w[0], taps)
        near = dot(t_ref[i], us[...])
        z_ref[:, cols] = near[:WIN] + near[WIN:]


def near_kernel(lanes, u_ref, t_ref, z_ref):
    length = u_ref.shape[0]
    for i, cols in spans(u_ref.shape[1] // lanes, lanes):
        near = dot(t_ref[i], u_ref[:, cols])
        z_ref[:, cols] = near[:length] + near[length:]


def final_kernel(
    lanes, scal, q_ref, z_ref, qt_ref, zt_ref, r_ref, rt_ref, st_ref, stt_ref,
    w_ref, b_ref, out_ref, mask_ref, w_scr, q_scr, z_scr, o_scr, sems,
):
    length = q_ref.shape[0]

    write_masks(mask_ref, WIN, scal[0], scal[1], length)
    copies = []
    for i, cols in spans(q_ref.shape[1] // lanes, lanes):
        k = i % w_scr.shape[0]
        ws, qs, zs = w_scr.at[k], q_scr.at[k], z_scr.at[k]
        zs[:WIN, :] = dot(rt_ref[i], stt_ref[:, cols])
        zs[WIN:, :] = dot(r_ref[i], st_ref[:, cols])
        for tile in tiles(lanes):
            here = slice(cols.start + tile.start, cols.start + tile.stop)
            w = weights_of(w_ref, here)
            prev = jnp.zeros((8, LANE), F32)
            for at in chunks(0, WIN) + chunks(WIN, WIN + length):
                if at.start < WIN:
                    q, z = qt_ref[at, here], zt_ref[at, here]
                else:
                    part = slice(at.start - WIN, at.stop - WIN)
                    q, z = q_ref[part, here], z_ref[part, here]
                y = (q * (z + zs[at, tile])).astype(BF).astype(F32)
                taps = taps_of(prev, y, mask_ref, at)
                prev = y[-8:]
                ws[at, tile] = (combine(w[1], taps) * combine(w[2], taps)).astype(BF)
                if at.start >= WIN:
                    qs[at.start - WIN : at.stop - WIN, tile] = combine(w[0], taps)
        span = b_ref.shape[2] // 2
        for first in range(0, length, span):
            rows = slice(first, first + span)
            z = dot(b_ref[i, rows, :], ws[WIN + first - span : WIN + first + span, :])
            o_scr[i, rows, :] = (qs[rows, :] * z).astype(BF)
        copies.append(pltpu.make_async_copy(o_scr.at[i], out_ref.at[:, cols], sems.at[i]))
        copies[-1].start()
    for copy in copies:
        copy.wait()


def per_device(inputs, bounds, feat_first, li_decay, li_residue, feat_second, mr_filter):
    length, channels = inputs.shape
    groups, modes = li_decay.shape
    lanes = channels // groups
    filter_len = mr_filter.shape[1]
    rows = filter_len + 3
    cut = length - rows + 2
    size = lax.axis_size("seq")

    def behind(array, by):
        return lax.ppermute(array, "seq", [(i, i + by) for i in range(size - by)])

    sm = pl.BlockSpec(memory_space=SMEM)
    whole = pl.BlockSpec(memory_space=pltpu.VMEM)
    params = pltpu.CompilerParams(vmem_limit_bytes=24 * 1024 * 1024)
    count = 2 if groups % 2 == 0 else 1
    steps, wide = groups // count, lanes * count

    hbm = pl.BlockSpec(memory_space=pl.ANY)
    held, held_first, held_decay, edge = pl.pallas_call(
        load_kernel,
        in_specs=[sm] + [hbm] * 3,
        out_specs=[whole] * 4,
        out_shape=[jax.ShapeDtypeStruct(a.shape, a.dtype) for a in (inputs, feat_first, li_decay)]
        + [jax.ShapeDtypeStruct((3, channels), BF)],
        scratch_shapes=[pltpu.SemaphoreType.DMA((3,))],
        compiler_params=pltpu.CompilerParams(vmem_limit_bytes=50 * 1024 * 1024),
        name="load",
    )(bounds, inputs, feat_first, li_decay)
    edge = behind(edge, 1)
    def block(*shape):
        return pl.BlockSpec(shape, lambda g: (0,) * (len(shape) - 1) + (g,))

    def table(*shape):
        return pl.BlockSpec((count,) + shape, lambda g: (g, 0, 0))

    def single(*shape):
        return pl.BlockSpec((None,) + shape, lambda g: (g, 0, 0))

    def fixed(*shape):
        return pl.BlockSpec(shape, lambda g: (0,) * len(shape))

    mine, part, q_own, u_own, scal = pl.pallas_call(
        functools.partial(states_kernel, cut, modes, lanes),
        in_specs=[sm] + [whole] * 4,
        out_specs=[whole] * 4 + [sm],
        out_shape=[
            jax.ShapeDtypeStruct((modes, channels + LANE), BF),
            jax.ShapeDtypeStruct((modes, channels), BF),
            jax.ShapeDtypeStruct((length, channels), F32),
            jax.ShapeDtypeStruct((length, channels), BF),
            jax.ShapeDtypeStruct((3,), jnp.int32),
        ],
        scratch_shapes=[
            pltpu.VMEM((2, length, LANE), F32),
        ],
        compiler_params=params,
        cost_estimate=pl.CostEstimate(flops=10**8, bytes_accessed=2**16, transcendentals=0),
        name="states",
    )(bounds, held, edge, held_first, held_decay)
    other = lax.ppermute(mine, "seq", [(i, i ^ 1) for i in range(size)])
    inputs_late, part, other = lax.optimization_barrier((held, part, other))
    message = jnp.concatenate([part, inputs_late[length - rows :]], 0)
    message, other = lax.optimization_barrier((message, other))
    tail = behind(message, 1)
    pair = pl.pallas_call(
        functools.partial(pair_kernel, modes, length),
        in_specs=[sm] + [whole] * 3,
        out_specs=whole,
        out_shape=jax.ShapeDtypeStruct((2 * modes, channels + LANE), BF),
        compiler_params=params,
        name="pair",
    )(scal, mine, other, held_decay)
    near = lax.ppermute(pair, "seq", [(i, i + 2) for i in range(0, size - 2, 2)])
    far = [
        lax.ppermute(pair[:modes], "seq", [(i, i + by) for i in range(0, size - by, 2)])
        for by in range(4, size, 2)
    ]
    state_shape = jax.ShapeDtypeStruct((modes, channels), F32)
    send, even_own, even_late = pl.pallas_call(
        functools.partial(carry_kernel, modes, length),
        in_specs=[whole] * (2 + len(far)),
        out_specs=[whole] * 3,
        out_shape=[jax.ShapeDtypeStruct((modes, channels), BF), state_shape, state_shape],
        compiler_params=params,
        name="carry",
    )(near, held_decay, *far)
    sent = lax.ppermute(send, "seq", [(i, i + 1) for i in range(0, size, 2)])
    own_state, win_state = pl.pallas_call(
        functools.partial(place_kernel, cut, modes, length),
        in_specs=[sm] + [whole] * 6,
        out_specs=[whole] * 2,
        out_shape=[jax.ShapeDtypeStruct((3 * modes, channels), BF)] * 2,
        compiler_params=params,
        name="place",
    )(scal, other, tail, sent, even_own, even_late, held_decay)

    shapes = [
        (2 * length, length), (2 * WIN, WIN), (length, 3 * modes), (WIN, 3 * modes),
        (length, 2 * filter_len),
    ]
    t_own, t_win, r_own, r_win, b_all = pl.pallas_call(
        functools.partial(tables_kernel, cut, modes, length),
        grid=(groups,),
        in_specs=[sm, fixed(groups, modes), fixed(groups, modes), single(1, filter_len)],
        out_specs=[single(*s) for s in shapes],
        out_shape=[jax.ShapeDtypeStruct((groups,) + s, BF) for s in shapes],
        compiler_params=params,
        cost_estimate=pl.CostEstimate(flops=10**8, bytes_accessed=2**16, transcendentals=0),
        name="tables",
    )(scal, li_decay, li_residue, mr_filter.reshape(groups, 1, filter_len))

    z_own = pl.pallas_call(
        functools.partial(near_kernel, lanes),
        in_specs=[whole] * 2,
        out_specs=whole,
        out_shape=jax.ShapeDtypeStruct((length, channels), F32),
        compiler_params=params,
        cost_estimate=pl.CostEstimate(flops=10**8, bytes_accessed=2**16, transcendentals=0),
        name="near",
    )(u_own, t_own)
    q_win, z_win = pl.pallas_call(
        functools.partial(tail_kernel, modes, length, lanes),
        in_specs=[sm] + [whole] * 3,
        out_specs=[whole] * 2,
        out_shape=[
            jax.ShapeDtypeStruct((WIN, channels), F32),
            jax.ShapeDtypeStruct((WIN, channels), F32),
        ],
        scratch_shapes=[
            pltpu.VMEM((2, WIN, LANE), F32), pltpu.VMEM((groups, 8 + WIN, lanes), F32),
            pltpu.VMEM((groups, WIN, lanes), BF),
        ],
        compiler_params=params,
        cost_estimate=pl.CostEstimate(flops=10**8, bytes_accessed=2**16, transcendentals=0),
        name="tail",
    )(scal, tail, held_first, t_win)
    full = WIN + length
    return pl.pallas_call(
        functools.partial(final_kernel, lanes),
        in_specs=[sm] + [whole] * 10,
        out_specs=pl.BlockSpec(memory_space=pl.ANY),
        out_shape=jax.ShapeDtypeStruct((length, channels), BF),
        scratch_shapes=[
            pltpu.VMEM((2, full, LANE), F32),
            pltpu.VMEM((count, full, lanes), BF), pltpu.VMEM((count, length, lanes), F32),
            pltpu.VMEM((count, full, lanes), F32), pltpu.VMEM((groups, length, lanes), BF),
            pltpu.SemaphoreType.DMA((groups,)),
        ],
        compiler_params=params,
        cost_estimate=pl.CostEstimate(flops=10**8, bytes_accessed=2**16, transcendentals=0),
        name="final",
    )(
        scal, q_own, z_own, q_win, z_win, r_own, r_win, own_state, win_state,
        feat_second, b_all,
    )


def solution(mesh):
    in_specs = (
        P(("groups", "seq"), "chan"),
        P(("groups", "seq")),
        P(None, None, "chan"),
        P("chan", None),
        P("chan", None),
        P(None, None, "chan"),
        P("chan", None),
    )
    out_specs = P(("groups", "seq"), "chan")
    return jax.shard_map(
        per_device, mesh=mesh, in_specs=in_specs, out_specs=out_specs, check_vma=False
    )
```

```python
import functools
import math

import jax
import jax.numpy as jnp
from jax import lax
from jax.experimental import pallas as pl
from jax.experimental.pallas import tpu as pltpu
from jax.sharding import PartitionSpec as P

F32 = jnp.float32
BF = jnp.bfloat16
WIN = 144
LANE = 128
CHUNK = 32
SMEM = pltpu.SMEM


def dot(a, b):
    return lax.dot_general(a, b, (((1,), (0,)), ((), ())), preferred_element_type=F32)


def iota(shape, dim):
    return lax.broadcasted_iota(jnp.int32, shape, dim)


def column(row):
    n = row.shape[1]
    return jnp.sum(
        jnp.where(iota((n, n), 0) == iota((n, n), 1), row, 0.0), axis=1, keepdims=True
    )


def one(cond):
    return jnp.where(cond, 1.0, 0.0).astype(BF)


def weights_of(w_ref, cols):
    return [[w_ref[b, o : o + 1, cols] for o in range(3)] for b in range(3)]


def combine(w, taps):
    return w[0] * taps[0] + w[1] * taps[1] + w[2] * taps[2]


def taps_at(ref, mask_ref, at, cols):
    rows = ref[at.start : at.stop + 8, cols]
    return (
        rows[8:],
        pltpu.roll(rows, 1, 0)[8:] * mask_ref[0, at, :],
        pltpu.roll(rows, 2, 0)[8:] * mask_ref[1, at, :],
    )


def taps_of(prev, rows, mask_ref, at):
    both = jnp.concatenate([prev, rows], 0)
    return (
        rows,
        pltpu.roll(both, 1, 0)[8:] * mask_ref[0, at, :],
        pltpu.roll(both, 2, 0)[8:] * mask_ref[1, at, :],
    )


def chunks(first, last, rows=CHUNK):
    return [slice(r, min(r + rows, last)) for r in range(first, last, rows)]


def tiles(lanes):
    return [slice(c, c + LANE) for c in range(0, lanes, LANE)]


def spans(count, lanes):
    return [(i, slice(i * lanes, (i + 1) * lanes)) for i in range(count)]


def write_masks(ref, offset, own, prior, length):
    rows = ref.shape[1]
    t = iota((rows, LANE), 0) - offset
    before = jnp.where(prior < length, prior, -length) - length
    one_back = (t != own) & (t != before)
    two_back = one_back & (t - 1 != own) & (t - 1 != before)
    ref[0] = jnp.where(one_back, 1.0, 0.0)
    ref[1] = jnp.where(two_back, 1.0, 0.0)


def split(v):
    hi = v.astype(BF)
    return hi, (v - hi.astype(F32)).astype(BF)


def load_kernel(bounds, x_ref, x_out, edge_out, sem):
    copy = pltpu.make_async_copy(x_ref, x_out, sem)
    copy.start()
    copy.wait()
    length, width = x_out.shape
    last = x_out[length - 16 :, :].astype(F32)[14:]
    own = jnp.full((1, width), bounds[0], jnp.int32).astype(F32)
    edge_out[...] = jnp.concatenate([last, own], 0).astype(BF)


def states_kernel(
    cut, modes, lanes, bounds, x_ref, edge_ref, w_ref, dec_ref, out_ref, part_ref, q_ref, u_ref,
    scal_ref, mask_ref,
):
    length, width = x_ref.shape
    own = bounds[0]
    place = lax.axis_index("seq")
    told = jnp.max(edge_ref[...].astype(F32)[2:3, :LANE]).astype(jnp.int32)
    prior = jnp.where(place == 0, length, told)
    scal_ref[0] = own
    scal_ref[1] = prior
    scal_ref[2] = place % 2
    write_masks(mask_ref, 0, own, prior, length)
    flag = jnp.full((modes, LANE), own, jnp.int32).astype(F32)
    out_ref[:, width:] = flag.astype(BF)

    p = iota((modes, length), 1)
    lag = (length - 1 - p).astype(F32)
    lag_cut = jnp.maximum(cut - 1 - p, 0).astype(F32)
    reach = (p >= own) | (own >= length)
    reach_cut = (p < cut) & ((p >= own) | (own >= cut))
    for i, cols in spans(width // lanes, lanes):
        for tile in tiles(lanes):
            here = slice(cols.start + tile.start, cols.start + tile.stop)
            w = weights_of(w_ref, here)
            edge = edge_ref[:, here].astype(F32)
            prev = jnp.concatenate([jnp.zeros((6, LANE), F32), edge[:2]], 0)
            for at in chunks(0, length):
                x = x_ref[at, here].astype(F32)
                taps = taps_of(prev, x, mask_ref, at)
                prev = x[-8:]
                u_ref[at, here] = (combine(w[1], taps) * combine(w[2], taps)).astype(BF)
                q_ref[at, here] = combine(w[0], taps)
        dec = column(dec_ref[i : i + 1, :])
        full = jnp.where(reach, jnp.exp(-dec * lag), 0.0)
        part = jnp.where(reach_cut, jnp.exp(-dec * lag_cut), 0.0)
        hi, lo = split(jnp.concatenate([full, part], 0))
        both = dot(jnp.concatenate([hi, lo], 0), u_ref[:, cols])
        state = both[: 2 * modes] + both[2 * modes :]
        out_ref[:, cols] = state[:modes].astype(BF)
        part_ref[:, cols] = state[modes:].astype(BF)


def pair_kernel(modes, length, scal, mine_ref, other_ref, dec_ref, out_ref):
    groups = dec_ref.shape[0]
    width = mine_ref.shape[1] - LANE
    lanes = width // groups
    even = scal[2] == 0
    end = slice(width, width + LANE)

    def pick(cols):
        a, b = mine_ref[:, cols].astype(F32), other_ref[:, cols].astype(F32)
        return jnp.where(even, a, b), jnp.where(even, b, a)

    top, low = slice(0, modes), slice(modes, 2 * modes)
    f_bound, s_bound = pick(end)
    free_f = jnp.where(f_bound >= length, 1.0, 0.0)
    free_s = jnp.where(s_bound >= length, 1.0, 0.0)
    out_ref[top, end] = (free_f * free_s).astype(BF)
    out_ref[low, end] = free_f.astype(BF)
    for g in range(groups):
        cols = slice(g * lanes, (g + 1) * lanes)
        dec = column(dec_ref[g : g + 1, :])
        first, second = pick(cols)
        out_ref[top, cols] = (second + jnp.exp(-dec * length) * free_s[:, :1] * first).astype(BF)
        out_ref[low, cols] = first.astype(BF)


def carry_kernel(modes, length, near_ref, dec_ref, *refs):
    far, (send_ref, own_ref, late_ref) = refs[:-3], refs[-3:]
    groups = dec_ref.shape[0]
    width = own_ref.shape[1]
    lanes = width // groups
    top, low = slice(0, modes), slice(modes, 2 * modes)
    near_free = near_ref[top, width : width + LANE].astype(F32)[:, :1]
    late_free = near_ref[low, width : width + LANE].astype(F32)[:, :1]
    far_free = [f[:, width : width + LANE].astype(F32)[:, :1] for f in far]
    for g in range(groups):
        cols = slice(g * lanes, (g + 1) * lanes)
        dec = column(dec_ref[g : g + 1, :])
        once = jnp.exp(-dec * length)
        pair = jnp.exp(-dec * (2 * length))
        behind = jnp.zeros((modes, lanes), F32)
        for f, free in zip(far[::-1], far_free[::-1]):
            behind = f[:, cols].astype(F32) + pair * free * behind
        whole = near_ref[top, cols].astype(F32) + pair * near_free * behind
        send_ref[:, cols] = whole.astype(BF)
        own_ref[:, cols] = whole
        late_ref[:, cols] = near_ref[low, cols].astype(F32) + once * late_free * behind


def place_kernel(
    cut, modes, length, scal, other_ref, part_ref, sent_ref, even_own, even_late, dec_ref,
    own_ref, win_ref,
):
    groups = dec_ref.shape[0]
    lanes = own_ref.shape[1] // groups
    even = scal[2] == 0
    prior = scal[1]
    pass_own = jnp.where(prior >= length, 1.0, 0.0)
    pass_cut = jnp.where(prior >= cut, 1.0, 0.0)
    for g in range(groups):
        cols = slice(g * lanes, (g + 1) * lanes)
        dec = column(dec_ref[g : g + 1, :])
        sent = sent_ref[:, cols].astype(F32)
        odd_own = other_ref[:, cols].astype(F32) + jnp.exp(-dec * length) * pass_own * sent
        before = jnp.where(even, even_late[:, cols], sent)
        own = jnp.where(even, even_own[:, cols], odd_own)
        win = part_ref[: dec_ref.shape[1], cols].astype(F32) + jnp.exp(-dec * cut) * pass_cut * before
        for ref, v in ((own_ref, own), (win_ref, win)):
            hi, lo = split(v)
            ref[:, cols] = jnp.concatenate([hi, lo, hi], 0)


def tables_kernel(cut, modes, length, scal, dec_ref, res_ref, mr_ref, *outs):
    t_own, t_win, r_own, r_win, b_all = outs
    g = pl.program_id(0)
    own, prior = scal[0], scal[1]
    wide = 2 * length
    base = length - WIN
    dec_row = dec_ref[pl.ds(g, 1), :]
    weight_row = res_ref[pl.ds(g, 1), :] * jnp.sqrt(
        jnp.maximum(1.0 - jnp.exp(-2.0 * dec_row), 0.0)
    ) / math.sqrt(modes)
    small = 2.0 * dec_row
    series = small * (1.0 - small * (0.5 - small * (1.0 / 6 - small * (1.0 / 24))))
    weight_row = jnp.where(
        small < 0.05,
        res_ref[pl.ds(g, 1), :] * jnp.sqrt(series) / math.sqrt(modes),
        weight_row,
    )
    dec, weight = column(dec_row), column(weight_row)
    back = iota((modes, wide), 1)
    back = jnp.where(back == 0, 0, wide - back).astype(F32)
    taps = jnp.sum(weight * jnp.exp(-dec * back), axis=0, keepdims=True)
    full = pltpu.roll(jnp.broadcast_to(taps, (length, wide)), 0, 1, stride=1, stride_axis=0)
    t, p = iota((length, length), 0), iota((length, length), 1)
    seen = (p <= t) & ((p >= own) == (t >= own))
    t_own[:length, :], t_own[length:, :] = split(jnp.where(seen, full[:, :length], 0.0))
    tw, pw = iota((WIN, WIN), 0) + base, iota((WIN, WIN), 1) + base
    seen = (pw <= tw) & (pw >= cut) & ((pw >= prior) == (tw >= prior))
    t_win[:WIN, :], t_win[WIN:, :] = split(jnp.where(seen, full[:WIN, :WIN], 0.0))

    tl = iota((modes, length), 1)
    rise = jnp.where(tl < own, weight * jnp.exp(-dec * (tl + 1).astype(F32)), 0.0)
    wl = tl + base
    lag = jnp.maximum(wl - cut + 1, 0)
    fits = (wl >= cut) & ((prior < cut) | (prior > wl))
    rise_w = jnp.where(fits, weight * jnp.exp(-dec * lag.astype(F32)), 0.0)
    for ref, v, rows in ((r_own, rise, length), (r_win, rise_w, WIN)):
        hi = v.astype(BF).astype(F32)
        stack = jnp.concatenate([hi, hi, v - hi, jnp.zeros((LANE - 3 * modes, length), F32)], 0)
        ref[...] = jnp.transpose(stack)[:rows, : 3 * modes].astype(BF)

    count = mr_ref.shape[1]
    o, n = iota((count, wide), 0), iota((count, wide), 1)
    back = dot(mr_ref[...], one(((n == 0) & (o == 0)) | ((n > 0) & (wide - n == o))))
    band = pltpu.roll(
        jnp.broadcast_to(back, (2 * count, wide)), 0, 1, stride=1, stride_axis=0
    )[count:, : 2 * count]
    for first in range(0, length, count):
        t = iota((count, 2 * count), 0) + first
        p = iota((count, 2 * count), 1) + (first - count)
        same = (p >= own) == (t >= own)
        early = (p >= 0) | (prior >= length) | (p + length >= prior)
        b_all[first : first + count, :] = jnp.where(same & early, band, 0.0).astype(BF)


def tail_kernel(
    modes, length, lanes, scal, tail_ref, w_ref, t_ref, q_ref, z_ref, mask_ref, x_scr, u_scr
):
    rows = tail_ref.shape[0] - modes

    write_masks(mask_ref, WIN, scal[0], scal[1], length)
    x_scr[:, : 8 + WIN - rows, :] = jnp.zeros(
        (x_scr.shape[0], 8 + WIN - rows, x_scr.shape[2]), F32
    )

    for i, cols in spans(tail_ref.shape[1] // lanes, lanes):
        scr, us = x_scr.at[i], u_scr.at[i]
        scr[8 + WIN - rows : 8 + WIN, :] = tail_ref[modes:, cols].astype(F32)
        for tile in tiles(lanes):
            here = slice(cols.start + tile.start, cols.start + tile.stop)
            w = weights_of(w_ref, here)
            for at in chunks(0, WIN):
                taps = taps_at(scr, mask_ref, at, tile)
                us[at, tile] = (combine(w[1], taps) * combine(w[2], taps)).astype(BF)
                q_ref[at, here] = combine(w[0], taps)
        near = dot(t_ref[i], us[...])
        z_ref[:, cols] = near[:WIN] + near[WIN:]


def near_kernel(lanes, u_ref, t_ref, z_ref):
    length = u_ref.shape[0]
    for i, cols in spans(u_ref.shape[1] // lanes, lanes):
        near = dot(t_ref[i], u_ref[:, cols])
        z_ref[:, cols] = near[:length] + near[length:]


def final_kernel(
    lanes, scal, q_ref, z_ref, qt_ref, zt_ref, r_ref, rt_ref, st_ref, stt_ref,
    w_ref, b_ref, out_ref, mask_ref, w_scr, q_scr, z_scr, o_scr, sems,
):
    length = q_ref.shape[0]

    write_masks(mask_ref, WIN, scal[0], scal[1], length)
    copies = []
    for i, cols in spans(q_ref.shape[1] // lanes, lanes):
        k = i % w_scr.shape[0]
        ws, qs, zs = w_scr.at[k], q_scr.at[k], z_scr.at[k]
        zs[:WIN, :] = dot(rt_ref[i], stt_ref[:, cols])
        zs[WIN:, :] = dot(r_ref[i], st_ref[:, cols])
        for tile in tiles(lanes):
            here = slice(cols.start + tile.start, cols.start + tile.stop)
            w = weights_of(w_ref, here)
            prev = jnp.zeros((8, LANE), F32)
            for at in chunks(0, WIN) + chunks(WIN, WIN + length):
                if at.start < WIN:
                    q, z = qt_ref[at, here], zt_ref[at, here]
                else:
                    part = slice(at.start - WIN, at.stop - WIN)
                    q, z = q_ref[part, here], z_ref[part, here]
                y = (q * (z + zs[at, tile])).astype(BF).astype(F32)
                taps = taps_of(prev, y, mask_ref, at)
                prev = y[-8:]
                ws[at, tile] = (combine(w[1], taps) * combine(w[2], taps)).astype(BF)
                if at.start >= WIN:
                    qs[at.start - WIN : at.stop - WIN, tile] = combine(w[0], taps)
        span = b_ref.shape[2] // 2
        for first in range(0, length, span):
            rows = slice(first, first + span)
            z = dot(b_ref[i, rows, :], ws[WIN + first - span : WIN + first + span, :])
            o_scr[i, rows, :] = (qs[rows, :] * z).astype(BF)
        copies.append(pltpu.make_async_copy(o_scr.at[i], out_ref.at[:, cols], sems.at[i]))
        copies[-1].start()
    for copy in copies:
        copy.wait()


def per_device(inputs, bounds, feat_first, li_decay, li_residue, feat_second, mr_filter):
    length, channels = inputs.shape
    groups, modes = li_decay.shape
    lanes = channels // groups
    filter_len = mr_filter.shape[1]
    rows = filter_len + 3
    cut = length - rows + 2
    size = lax.axis_size("seq")

    def behind(array, by):
        return lax.ppermute(array, "seq", [(i, i + by) for i in range(size - by)])

    sm = pl.BlockSpec(memory_space=SMEM)
    whole = pl.BlockSpec(memory_space=pltpu.VMEM)
    params = pltpu.CompilerParams(vmem_limit_bytes=24 * 1024 * 1024)
    count = 2 if groups % 2 == 0 else 1
    steps, wide = groups // count, lanes * count

    hbm = pl.BlockSpec(memory_space=pl.ANY)
    held, edge = pl.pallas_call(
        load_kernel,
        in_specs=[sm, hbm],
        out_specs=[whole] * 2,
        out_shape=[
            jax.ShapeDtypeStruct(inputs.shape, BF), jax.ShapeDtypeStruct((3, channels), BF),
        ],
        scratch_shapes=[pltpu.SemaphoreType.DMA],
        compiler_params=pltpu.CompilerParams(vmem_limit_bytes=50 * 1024 * 1024),
        name="load",
    )(bounds, inputs)
    edge = behind(edge, 1)
    def block(*shape):
        return pl.BlockSpec(shape, lambda g: (0,) * (len(shape) - 1) + (g,))

    def table(*shape):
        return pl.BlockSpec((count,) + shape, lambda g: (g, 0, 0))

    def single(*shape):
        return pl.BlockSpec((None,) + shape, lambda g: (g, 0, 0))

    def fixed(*shape):
        return pl.BlockSpec(shape, lambda g: (0,) * len(shape))

    mine, part, q_own, u_own, scal = pl.pallas_call(
        functools.partial(states_kernel, cut, modes, lanes),
        in_specs=[sm] + [whole] * 4,
        out_specs=[whole] * 4 + [sm],
        out_shape=[
            jax.ShapeDtypeStruct((modes, channels + LANE), BF),
            jax.ShapeDtypeStruct((modes, channels), BF),
            jax.ShapeDtypeStruct((length, channels), F32),
            jax.ShapeDtypeStruct((length, channels), BF),
            jax.ShapeDtypeStruct((3,), jnp.int32),
        ],
        scratch_shapes=[
            pltpu.VMEM((2, length, LANE), F32),
        ],
        compiler_params=params,
        cost_estimate=pl.CostEstimate(flops=10**8, bytes_accessed=2**16, transcendentals=0),
        name="states",
    )(bounds, held, edge, feat_first, li_decay)
    other = lax.ppermute(mine, "seq", [(i, i ^ 1) for i in range(size)])
    inputs_late, part, other = lax.optimization_barrier((held, part, other))
    message = jnp.concatenate([part, inputs_late[length - rows :]], 0)
    message, other = lax.optimization_barrier((message, other))
    tail = behind(message, 1)
    pair = pl.pallas_call(
        functools.partial(pair_kernel, modes, length),
        in_specs=[sm] + [whole] * 3,
        out_specs=whole,
        out_shape=jax.ShapeDtypeStruct((2 * modes, channels + LANE), BF),
        compiler_params=params,
        name="pair",
    )(scal, mine, other, li_decay)
    near = lax.ppermute(pair, "seq", [(i, i + 2) for i in range(0, size - 2, 2)])
    far = [
        lax.ppermute(pair[:modes], "seq", [(i, i + by) for i in range(0, size - by, 2)])
        for by in range(4, size, 2)
    ]
    state_shape = jax.ShapeDtypeStruct((modes, channels), F32)
    send, even_own, even_late = pl.pallas_call(
        functools.partial(carry_kernel, modes, length),
        in_specs=[whole] * (2 + len(far)),
        out_specs=[whole] * 3,
        out_shape=[jax.ShapeDtypeStruct((modes, channels), BF), state_shape, state_shape],
        compiler_params=params,
        name="carry",
    )(near, li_decay, *far)
    sent = lax.ppermute(send, "seq", [(i, i + 1) for i in range(0, size, 2)])
    own_state, win_state = pl.pallas_call(
        functools.partial(place_kernel, cut, modes, length),
        in_specs=[sm] + [whole] * 6,
        out_specs=[whole] * 2,
        out_shape=[jax.ShapeDtypeStruct((3 * modes, channels), BF)] * 2,
        compiler_params=params,
        name="place",
    )(scal, other, tail, sent, even_own, even_late, li_decay)

    shapes = [
        (2 * length, length), (2 * WIN, WIN), (length, 3 * modes), (WIN, 3 * modes),
        (length, 2 * filter_len),
    ]
    t_own, t_win, r_own, r_win, b_all = pl.pallas_call(
        functools.partial(tables_kernel, cut, modes, length),
        grid=(groups,),
        in_specs=[sm, fixed(groups, modes), fixed(groups, modes), single(1, filter_len)],
        out_specs=[single(*s) for s in shapes],
        out_shape=[jax.ShapeDtypeStruct((groups,) + s, BF) for s in shapes],
        compiler_params=params,
        cost_estimate=pl.CostEstimate(flops=10**8, bytes_accessed=2**16, transcendentals=0),
        name="tables",
    )(scal, li_decay, li_residue, mr_filter.reshape(groups, 1, filter_len))

    z_own = pl.pallas_call(
        functools.partial(near_kernel, lanes),
        in_specs=[whole] * 2,
        out_specs=whole,
        out_shape=jax.ShapeDtypeStruct((length, channels), F32),
        compiler_params=params,
        cost_estimate=pl.CostEstimate(flops=10**8, bytes_accessed=2**16, transcendentals=0),
        name="near",
    )(u_own, t_own)
    q_win, z_win = pl.pallas_call(
        functools.partial(tail_kernel, modes, length, lanes),
        in_specs=[sm] + [whole] * 3,
        out_specs=[whole] * 2,
        out_shape=[
            jax.ShapeDtypeStruct((WIN, channels), F32),
            jax.ShapeDtypeStruct((WIN, channels), F32),
        ],
        scratch_shapes=[
            pltpu.VMEM((2, WIN, LANE), F32), pltpu.VMEM((groups, 8 + WIN, lanes), F32),
            pltpu.VMEM((groups, WIN, lanes), BF),
        ],
        compiler_params=params,
        cost_estimate=pl.CostEstimate(flops=10**8, bytes_accessed=2**16, transcendentals=0),
        name="tail",
    )(scal, tail, feat_first, t_win)
    full = WIN + length
    return pl.pallas_call(
        functools.partial(final_kernel, lanes),
        in_specs=[sm] + [whole] * 10,
        out_specs=pl.BlockSpec(memory_space=pl.ANY),
        out_shape=jax.ShapeDtypeStruct((length, channels), BF),
        scratch_shapes=[
            pltpu.VMEM((2, full, LANE), F32),
            pltpu.VMEM((count, full, lanes), BF), pltpu.VMEM((count, length, lanes), F32),
            pltpu.VMEM((count, full, lanes), F32), pltpu.VMEM((groups, length, lanes), BF),
            pltpu.SemaphoreType.DMA((groups,)),
        ],
        compiler_params=params,
        cost_estimate=pl.CostEstimate(flops=10**8, bytes_accessed=2**16, transcendentals=0),
        name="final",
    )(
        scal, q_own, z_own, q_win, z_win, r_own, r_win, own_state, win_state,
        feat_second, b_all,
    )


def solution(mesh):
    in_specs = (
        P(("groups", "seq"), "chan"),
        P(("groups", "seq")),
        P(None, None, "chan"),
        P("chan", None),
        P("chan", None),
        P(None, None, "chan"),
        P("chan", None),
    )
    out_specs = P(("groups", "seq"), "chan")
    return jax.shard_map(
        per_device, mesh=mesh, in_specs=in_specs, out_specs=out_specs, check_vma=False
    )
```

```python
import functools
import math

import jax
import jax.numpy as jnp
from jax import lax
from jax.experimental import pallas as pl
from jax.experimental.pallas import tpu as pltpu
from jax.sharding import PartitionSpec as P

F32 = jnp.float32
BF = jnp.bfloat16
WIN = 144
LANE = 128
CHUNK = 32
SMEM = pltpu.SMEM


def dot(a, b):
    return lax.dot_general(a, b, (((1,), (0,)), ((), ())), preferred_element_type=F32)


def iota(shape, dim):
    return lax.broadcasted_iota(jnp.int32, shape, dim)


def column(row):
    n = row.shape[1]
    return jnp.sum(
        jnp.where(iota((n, n), 0) == iota((n, n), 1), row, 0.0), axis=1, keepdims=True
    )


def one(cond):
    return jnp.where(cond, 1.0, 0.0).astype(BF)


def weights_of(w_ref, cols):
    return [[w_ref[b, o : o + 1, cols] for o in range(3)] for b in range(3)]


def combine(w, taps):
    return w[0] * taps[0] + w[1] * taps[1] + w[2] * taps[2]


def taps_at(ref, mask_ref, at, cols):
    rows = ref[at.start : at.stop + 8, cols]
    return (
        rows[8:],
        pltpu.roll(rows, 1, 0)[8:] * mask_ref[0, at, :],
        pltpu.roll(rows, 2, 0)[8:] * mask_ref[1, at, :],
    )


def taps_of(prev, rows, mask_ref, at):
    both = jnp.concatenate([prev, rows], 0)
    return (
        rows,
        pltpu.roll(both, 1, 0)[8:] * mask_ref[0, at, :],
        pltpu.roll(both, 2, 0)[8:] * mask_ref[1, at, :],
    )


def chunks(first, last, rows=CHUNK):
    return [slice(r, min(r + rows, last)) for r in range(first, last, rows)]


def tiles(lanes):
    return [slice(c, c + LANE) for c in range(0, lanes, LANE)]


def spans(count, lanes):
    return [(i, slice(i * lanes, (i + 1) * lanes)) for i in range(count)]


def write_masks(ref, offset, own, prior, length):
    rows = ref.shape[1]
    t = iota((rows, LANE), 0) - offset
    before = jnp.where(prior < length, prior, -length) - length
    one_back = (t != own) & (t != before)
    two_back = one_back & (t - 1 != own) & (t - 1 != before)
    ref[0] = jnp.where(one_back, 1.0, 0.0)
    ref[1] = jnp.where(two_back, 1.0, 0.0)


def split(v):
    hi = v.astype(BF)
    return hi, (v - hi.astype(F32)).astype(BF)


def load_kernel(bounds, x_ref, x_out, edge_out, sem):
    copy = pltpu.make_async_copy(x_ref, x_out, sem)
    copy.start()
    copy.wait()
    length, width = x_out.shape
    last = x_out[length - 16 :, :].astype(F32)[14:]
    own = jnp.full((1, width), bounds[0], jnp.int32).astype(F32)
    edge_out[...] = jnp.concatenate([last, own], 0).astype(BF)


def states_kernel(
    cut, modes, lanes, bounds, x_ref, edge_ref, w_ref, dec_ref, out_ref, part_ref, q_ref, u_ref,
    scal_ref, mask_ref,
):
    length, width = x_ref.shape
    own = bounds[0]
    place = lax.axis_index("seq")
    told = jnp.max(edge_ref[...].astype(F32)[2:3, :LANE]).astype(jnp.int32)
    prior = jnp.where(place == 0, length, told)
    scal_ref[0] = own
    scal_ref[1] = prior
    scal_ref[2] = place % 2
    write_masks(mask_ref, 0, own, prior, length)
    flag = jnp.full((modes, LANE), own, jnp.int32).astype(F32)
    out_ref[:, width:] = flag.astype(BF)

    p = iota((modes, length), 1)
    lag = (length - 1 - p).astype(F32)
    lag_cut = jnp.maximum(cut - 1 - p, 0).astype(F32)
    reach = (p >= own) | (own >= length)
    reach_cut = (p < cut) & ((p >= own) | (own >= cut))
    for i, cols in spans(width // lanes, lanes):
        for tile in tiles(lanes):
            here = slice(cols.start + tile.start, cols.start + tile.stop)
            w = weights_of(w_ref, here)
            edge = edge_ref[:, here].astype(F32)
            prev = jnp.concatenate([jnp.zeros((6, LANE), F32), edge[:2]], 0)
            for at in chunks(0, length):
                x = x_ref[at, here].astype(F32)
                taps = taps_of(prev, x, mask_ref, at)
                prev = x[-8:]
                u_ref[at, here] = (combine(w[1], taps) * combine(w[2], taps)).astype(BF)
                q_ref[at, here] = combine(w[0], taps)
        dec = column(dec_ref[i : i + 1, :])
        full = jnp.where(reach, jnp.exp(-dec * lag), 0.0)
        part = jnp.where(reach_cut, jnp.exp(-dec * lag_cut), 0.0)
        hi, lo = split(jnp.concatenate([full, part], 0))
        both = dot(jnp.concatenate([hi, lo], 0), u_ref[:, cols])
        state = both[: 2 * modes] + both[2 * modes :]
        out_ref[:, cols] = state[:modes].astype(BF)
        part_ref[:, cols] = state[modes:].astype(BF)


def pair_kernel(modes, length, scal, mine_ref, other_ref, dec_ref, out_ref):
    groups = dec_ref.shape[0]
    width = mine_ref.shape[1] - LANE
    lanes = width // groups
    even = scal[2] == 0
    end = slice(width, width + LANE)

    def pick(cols):
        a, b = mine_ref[:, cols].astype(F32), other_ref[:, cols].astype(F32)
        return jnp.where(even, a, b), jnp.where(even, b, a)

    top, low = slice(0, modes), slice(modes, 2 * modes)
    f_bound, s_bound = pick(end)
    free_f = jnp.where(f_bound >= length, 1.0, 0.0)
    free_s = jnp.where(s_bound >= length, 1.0, 0.0)
    out_ref[top, end] = (free_f * free_s).astype(BF)
    out_ref[low, end] = free_f.astype(BF)
    for g in range(groups):
        cols = slice(g * lanes, (g + 1) * lanes)
        dec = column(dec_ref[g : g + 1, :])
        first, second = pick(cols)
        out_ref[top, cols] = (second + jnp.exp(-dec * length) * free_s[:, :1] * first).astype(BF)
        out_ref[low, cols] = first.astype(BF)


def carry_kernel(modes, length, near_ref, dec_ref, *refs):
    far, (send_ref, own_ref, late_ref) = refs[:-3], refs[-3:]
    groups = dec_ref.shape[0]
    width = own_ref.shape[1]
    lanes = width // groups
    top, low = slice(0, modes), slice(modes, 2 * modes)
    near_free = near_ref[top, width : width + LANE].astype(F32)[:, :1]
    late_free = near_ref[low, width : width + LANE].astype(F32)[:, :1]
    far_free = [f[:, width : width + LANE].astype(F32)[:, :1] for f in far]
    for g in range(groups):
        cols = slice(g * lanes, (g + 1) * lanes)
        dec = column(dec_ref[g : g + 1, :])
        once = jnp.exp(-dec * length)
        pair = jnp.exp(-dec * (2 * length))
        behind = jnp.zeros((modes, lanes), F32)
        for f, free in zip(far[::-1], far_free[::-1]):
            behind = f[:, cols].astype(F32) + pair * free * behind
        whole = near_ref[top, cols].astype(F32) + pair * near_free * behind
        send_ref[:, cols] = whole.astype(BF)
        own_ref[:, cols] = whole
        late_ref[:, cols] = near_ref[low, cols].astype(F32) + once * late_free * behind


def place_kernel(
    cut, modes, length, scal, other_ref, part_ref, sent_ref, even_own, even_late, dec_ref,
    own_ref, win_ref,
):
    groups = dec_ref.shape[0]
    lanes = own_ref.shape[1] // groups
    even = scal[2] == 0
    prior = scal[1]
    pass_own = jnp.where(prior >= length, 1.0, 0.0)
    pass_cut = jnp.where(prior >= cut, 1.0, 0.0)
    for g in range(groups):
        cols = slice(g * lanes, (g + 1) * lanes)
        dec = column(dec_ref[g : g + 1, :])
        sent = sent_ref[:, cols].astype(F32)
        odd_own = other_ref[:, cols].astype(F32) + jnp.exp(-dec * length) * pass_own * sent
        before = jnp.where(even, even_late[:, cols], sent)
        own = jnp.where(even, even_own[:, cols], odd_own)
        win = part_ref[: dec_ref.shape[1], cols].astype(F32) + jnp.exp(-dec * cut) * pass_cut * before
        for ref, v in ((own_ref, own), (win_ref, win)):
            hi, lo = split(v)
            ref[:, cols] = jnp.concatenate([hi, lo, hi], 0)


def tables_kernel(cut, modes, length, scal, dec_ref, res_ref, mr_ref, *outs):
    t_own, t_win, r_own, r_win, b_all = outs
    g = pl.program_id(0)
    own, prior = scal[0], scal[1]
    wide = 2 * length
    base = length - WIN
    dec_row = dec_ref[pl.ds(g, 1), :]
    weight_row = res_ref[pl.ds(g, 1), :] * jnp.sqrt(
        jnp.maximum(1.0 - jnp.exp(-2.0 * dec_row), 0.0)
    ) / math.sqrt(modes)
    small = 2.0 * dec_row
    series = small * (1.0 - small * (0.5 - small * (1.0 / 6 - small * (1.0 / 24))))
    weight_row = jnp.where(
        small < 0.05,
        res_ref[pl.ds(g, 1), :] * jnp.sqrt(series) / math.sqrt(modes),
        weight_row,
    )
    dec, weight = column(dec_row), column(weight_row)
    back = iota((modes, wide), 1)
    back = jnp.where(back == 0, 0, wide - back).astype(F32)
    taps = jnp.sum(weight * jnp.exp(-dec * back), axis=0, keepdims=True)
    full = pltpu.roll(jnp.broadcast_to(taps, (length, wide)), 0, 1, stride=1, stride_axis=0)
    t, p = iota((length, length), 0), iota((length, length), 1)
    seen = (p <= t) & ((p >= own) == (t >= own))
    t_own[:length, :], t_own[length:, :] = split(jnp.where(seen, full[:, :length], 0.0))
    tw, pw = iota((WIN, WIN), 0) + base, iota((WIN, WIN), 1) + base
    seen = (pw <= tw) & (pw >= cut) & ((pw >= prior) == (tw >= prior))
    t_win[:WIN, :], t_win[WIN:, :] = split(jnp.where(seen, full[:WIN, :WIN], 0.0))

    tl = iota((modes, length), 1)
    rise = jnp.where(tl < own, weight * jnp.exp(-dec * (tl + 1).astype(F32)), 0.0)
    wl = tl + base
    lag = jnp.maximum(wl - cut + 1, 0)
    fits = (wl >= cut) & ((prior < cut) | (prior > wl))
    rise_w = jnp.where(fits, weight * jnp.exp(-dec * lag.astype(F32)), 0.0)
    for ref, v, rows in ((r_own, rise, length), (r_win, rise_w, WIN)):
        hi = v.astype(BF).astype(F32)
        stack = jnp.concatenate([hi, hi, v - hi, jnp.zeros((LANE - 3 * modes, length), F32)], 0)
        ref[...] = jnp.transpose(stack)[:rows, : 3 * modes].astype(BF)

    count = mr_ref.shape[1]
    o, n = iota((count, wide), 0), iota((count, wide), 1)
    back = dot(mr_ref[...], one(((n == 0) & (o == 0)) | ((n > 0) & (wide - n == o))))
    band = pltpu.roll(
        jnp.broadcast_to(back, (2 * count, wide)), 0, 1, stride=1, stride_axis=0
    )[count:, : 2 * count]
    for first in range(0, length, count):
        t = iota((count, 2 * count), 0) + first
        p = iota((count, 2 * count), 1) + (first - count)
        same = (p >= own) == (t >= own)
        early = (p >= 0) | (prior >= length) | (p + length >= prior)
        b_all[first : first + count, :] = jnp.where(same & early, band, 0.0).astype(BF)


def tail_kernel(
    modes, lanes, tail_ref, w_ref, t_ref, mask_ref, q_ref, z_ref, x_scr, u_scr
):
    rows = tail_ref.shape[0] - modes

    x_scr[:, : 8 + WIN - rows, :] = jnp.zeros(
        (x_scr.shape[0], 8 + WIN - rows, x_scr.shape[2]), F32
    )

    for i, cols in spans(tail_ref.shape[1] // lanes, lanes):
        scr, us = x_scr.at[i], u_scr.at[i]
        scr[8 + WIN - rows : 8 + WIN, :] = tail_ref[modes:, cols].astype(F32)
        for tile in tiles(lanes):
            here = slice(cols.start + tile.start, cols.start + tile.stop)
            w = weights_of(w_ref, here)
            for at in chunks(0, WIN):
                taps = taps_at(scr, mask_ref, at, tile)
                us[at, tile] = (combine(w[1], taps) * combine(w[2], taps)).astype(BF)
                q_ref[at, here] = combine(w[0], taps)
        near = dot(t_ref[i], us[...])
        z_ref[:, cols] = near[:WIN] + near[WIN:]


def near_kernel(lanes, scal, u_ref, t_ref, z_ref, mask_ref):
    length = u_ref.shape[0]
    write_masks(mask_ref, WIN, scal[0], scal[1], length)
    for i, cols in spans(u_ref.shape[1] // lanes, lanes):
        near = dot(t_ref[i], u_ref[:, cols])
        z_ref[:, cols] = near[:length] + near[length:]


def final_kernel(
    lanes, q_ref, z_ref, qt_ref, zt_ref, r_ref, rt_ref, st_ref, stt_ref,
    w_ref, b_ref, mask_ref, out_ref, w_scr, q_scr, z_scr, o_scr, sems,
):
    length = q_ref.shape[0]

    copies = []
    for i, cols in spans(q_ref.shape[1] // lanes, lanes):
        k = i % w_scr.shape[0]
        ws, qs, zs = w_scr.at[k], q_scr.at[k], z_scr.at[k]
        zs[:WIN, :] = dot(rt_ref[i], stt_ref[:, cols])
        zs[WIN:, :] = dot(r_ref[i], st_ref[:, cols])
        for tile in tiles(lanes):
            here = slice(cols.start + tile.start, cols.start + tile.stop)
            w = weights_of(w_ref, here)
            prev = jnp.zeros((8, LANE), F32)
            for at in chunks(0, WIN) + chunks(WIN, WIN + length):
                if at.start < WIN:
                    q, z = qt_ref[at, here], zt_ref[at, here]
                else:
                    part = slice(at.start - WIN, at.stop - WIN)
                    q, z = q_ref[part, here], z_ref[part, here]
                y = (q * (z + zs[at, tile])).astype(BF).astype(F32)
                taps = taps_of(prev, y, mask_ref, at)
                prev = y[-8:]
                ws[at, tile] = (combine(w[1], taps) * combine(w[2], taps)).astype(BF)
                if at.start >= WIN:
                    qs[at.start - WIN : at.stop - WIN, tile] = combine(w[0], taps)
        span = b_ref.shape[2] // 2
        for first in range(0, length, span):
            rows = slice(first, first + span)
            z = dot(b_ref[i, rows, :], ws[WIN + first - span : WIN + first + span, :])
            o_scr[i, rows, :] = (qs[rows, :] * z).astype(BF)
        copies.append(pltpu.make_async_copy(o_scr.at[i], out_ref.at[:, cols], sems.at[i]))
        copies[-1].start()
    for copy in copies:
        copy.wait()


def per_device(inputs, bounds, feat_first, li_decay, li_residue, feat_second, mr_filter):
    length, channels = inputs.shape
    groups, modes = li_decay.shape
    lanes = channels // groups
    filter_len = mr_filter.shape[1]
    rows = filter_len + 3
    cut = length - rows + 2
    size = lax.axis_size("seq")

    def behind(array, by):
        return lax.ppermute(array, "seq", [(i, i + by) for i in range(size - by)])

    sm = pl.BlockSpec(memory_space=SMEM)
    whole = pl.BlockSpec(memory_space=pltpu.VMEM)
    params = pltpu.CompilerParams(vmem_limit_bytes=24 * 1024 * 1024)
    count = 2 if groups % 2 == 0 else 1
    steps, wide = groups // count, lanes * count

    hbm = pl.BlockSpec(memory_space=pl.ANY)
    held, edge = pl.pallas_call(
        load_kernel,
        in_specs=[sm, hbm],
        out_specs=[whole] * 2,
        out_shape=[
            jax.ShapeDtypeStruct(inputs.shape, BF), jax.ShapeDtypeStruct((3, channels), BF),
        ],
        scratch_shapes=[pltpu.SemaphoreType.DMA],
        compiler_params=pltpu.CompilerParams(vmem_limit_bytes=50 * 1024 * 1024),
        name="load",
    )(bounds, inputs)
    edge = behind(edge, 1)
    def block(*shape):
        return pl.BlockSpec(shape, lambda g: (0,) * (len(shape) - 1) + (g,))

    def table(*shape):
        return pl.BlockSpec((count,) + shape, lambda g: (g, 0, 0))

    def single(*shape):
        return pl.BlockSpec((None,) + shape, lambda g: (g, 0, 0))

    def fixed(*shape):
        return pl.BlockSpec(shape, lambda g: (0,) * len(shape))

    mine, part, q_own, u_own, scal = pl.pallas_call(
        functools.partial(states_kernel, cut, modes, lanes),
        in_specs=[sm] + [whole] * 4,
        out_specs=[whole] * 4 + [sm],
        out_shape=[
            jax.ShapeDtypeStruct((modes, channels + LANE), BF),
            jax.ShapeDtypeStruct((modes, channels), BF),
            jax.ShapeDtypeStruct((length, channels), F32),
            jax.ShapeDtypeStruct((length, channels), BF),
            jax.ShapeDtypeStruct((3,), jnp.int32),
        ],
        scratch_shapes=[
            pltpu.VMEM((2, length, LANE), F32),
        ],
        compiler_params=params,
        cost_estimate=pl.CostEstimate(flops=10**8, bytes_accessed=2**16, transcendentals=0),
        name="states",
    )(bounds, held, edge, feat_first, li_decay)
    other = lax.ppermute(mine, "seq", [(i, i ^ 1) for i in range(size)])
    inputs_late, part, other = lax.optimization_barrier((held, part, other))
    message = jnp.concatenate([part, inputs_late[length - rows :]], 0)
    message, other = lax.optimization_barrier((message, other))
    tail = behind(message, 1)
    pair = pl.pallas_call(
        functools.partial(pair_kernel, modes, length),
        in_specs=[sm] + [whole] * 3,
        out_specs=whole,
        out_shape=jax.ShapeDtypeStruct((2 * modes, channels + LANE), BF),
        compiler_params=params,
        name="pair",
    )(scal, mine, other, li_decay)
    near = lax.ppermute(pair, "seq", [(i, i + 2) for i in range(0, size - 2, 2)])
    far = [
        lax.ppermute(pair[:modes], "seq", [(i, i + by) for i in range(0, size - by, 2)])
        for by in range(4, size, 2)
    ]
    state_shape = jax.ShapeDtypeStruct((modes, channels), F32)
    send, even_own, even_late = pl.pallas_call(
        functools.partial(carry_kernel, modes, length),
        in_specs=[whole] * (2 + len(far)),
        out_specs=[whole] * 3,
        out_shape=[jax.ShapeDtypeStruct((modes, channels), BF), state_shape, state_shape],
        compiler_params=params,
        name="carry",
    )(near, li_decay, *far)
    sent = lax.ppermute(send, "seq", [(i, i + 1) for i in range(0, size, 2)])
    own_state, win_state = pl.pallas_call(
        functools.partial(place_kernel, cut, modes, length),
        in_specs=[sm] + [whole] * 6,
        out_specs=[whole] * 2,
        out_shape=[jax.ShapeDtypeStruct((3 * modes, channels), BF)] * 2,
        compiler_params=params,
        name="place",
    )(scal, other, tail, sent, even_own, even_late, li_decay)

    shapes = [
        (2 * length, length), (2 * WIN, WIN), (length, 3 * modes), (WIN, 3 * modes),
        (length, 2 * filter_len),
    ]
    t_own, t_win, r_own, r_win, b_all = pl.pallas_call(
        functools.partial(tables_kernel, cut, modes, length),
        grid=(groups,),
        in_specs=[sm, fixed(groups, modes), fixed(groups, modes), single(1, filter_len)],
        out_specs=[single(*s) for s in shapes],
        out_shape=[jax.ShapeDtypeStruct((groups,) + s, BF) for s in shapes],
        compiler_params=params,
        cost_estimate=pl.CostEstimate(flops=10**8, bytes_accessed=2**16, transcendentals=0),
        name="tables",
    )(scal, li_decay, li_residue, mr_filter.reshape(groups, 1, filter_len))

    full = WIN + length
    z_own, masks = pl.pallas_call(
        functools.partial(near_kernel, lanes),
        in_specs=[sm] + [whole] * 2,
        out_specs=[whole] * 2,
        out_shape=[
            jax.ShapeDtypeStruct((length, channels), F32),
            jax.ShapeDtypeStruct((2, full, LANE), F32),
        ],
        compiler_params=params,
        cost_estimate=pl.CostEstimate(flops=10**8, bytes_accessed=2**16, transcendentals=0),
        name="near",
    )(scal, u_own, t_own)
    q_win, z_win = pl.pallas_call(
        functools.partial(tail_kernel, modes, lanes),
        in_specs=[whole] * 4,
        out_specs=[whole] * 2,
        out_shape=[
            jax.ShapeDtypeStruct((WIN, channels), F32),
            jax.ShapeDtypeStruct((WIN, channels), F32),
        ],
        scratch_shapes=[
            pltpu.VMEM((groups, 8 + WIN, lanes), F32),
            pltpu.VMEM((groups, WIN, lanes), BF),
        ],
        compiler_params=params,
        cost_estimate=pl.CostEstimate(flops=10**8, bytes_accessed=2**16, transcendentals=0),
        name="tail",
    )(tail, feat_first, t_win, masks)
    return pl.pallas_call(
        functools.partial(final_kernel, lanes),
        in_specs=[whole] * 11,
        out_specs=pl.BlockSpec(memory_space=pl.ANY),
        out_shape=jax.ShapeDtypeStruct((length, channels), BF),
        scratch_shapes=[
            pltpu.VMEM((count, full, lanes), BF), pltpu.VMEM((count, length, lanes), F32),
            pltpu.VMEM((count, full, lanes), F32), pltpu.VMEM((groups, length, lanes), BF),
            pltpu.SemaphoreType.DMA((groups,)),
        ],
        compiler_params=params,
        cost_estimate=pl.CostEstimate(flops=10**8, bytes_accessed=2**16, transcendentals=0),
        name="final",
    )(
        q_own, z_own, q_win, z_win, r_own, r_win, own_state, win_state,
        feat_second, b_all, masks,
    )


def solution(mesh):
    in_specs = (
        P(("groups", "seq"), "chan"),
        P(("groups", "seq")),
        P(None, None, "chan"),
        P("chan", None),
        P("chan", None),
        P(None, None, "chan"),
        P("chan", None),
    )
    out_specs = P(("groups", "seq"), "chan")
    return jax.shard_map(
        per_device, mesh=mesh, in_specs=in_specs, out_specs=out_specs, check_vma=False
    )
```
